128 devices in a mesh: dp: 8 (over x, core), seq: 16 (over y, z).
Axes of the slice: x: 4, y: 4, z: 4, core: 2. Of those that a mesh axis runs over, the one named last changes fastest.
Arguments:
- values: bfloat16 [8, 8192, 4096], P('dp', 'seq'), may hold values from -6 to 6
- gate_one: bfloat16 [8, 8192, 4096], P('dp', 'seq'), may hold values from -6 to 6
- gate_two: bfloat16 [8, 8192, 4096], P('dp', 'seq'), may hold values from -6 to 6
- gate_three: bfloat16 [8, 8192, 4096], P('dp', 'seq'), may hold values from -6 to 6
- genome_blocks: int32 [8, 4], P('dp'), may hold values from 1 to 32, 64 in all within a row
- short_taps: bfloat16 [7, 4096], replicated, may hold values from -2 to 2
- medium_taps: bfloat16 [128, 4096], P(None, 'dp'), may hold values from -0.5 to 0.5
- decay_rate: float32 [4096, 16], replicated, may hold values from 8.138021e-06 to 0.25, as said below
- residue: float32 [4096, 16], replicated, may hold values from -1.5 to 1.5
- long_skip: float32 [4096], replicated, may hold values from -1.75 to 1.75
Outputs:
- mixed: bfloat16 [8, 8192, 4096], P('dp', 'seq')
The draws below stay inside these ranges and needn't reach their ends.
Inputs may be any that keep to these rules, and one draw needn't show every extreme that they name: `genome_blocks`: each row's 4 genome lengths, counted in blocks of 128 tokens, are positive and sum to 64; the longest is exactly 32. `decay_rate`: positive decay rates.
All inputs are finite; a program needn't handle non-finite values.
Results may differ from the reference program's by a relative error of at most 0.0085.
Values may be sent and summed in bfloat16 or wider, within the bound.
A program may use at most 256 MiB of HBM per device.

```python
import math
import jax
import jax.numpy as jnp
import numpy as np
from jax import lax

C = 4096
MODES = 16
SHORT_TAPS = 7
MED_TAPS = 128
BLOCK = 128
GENOMES = 4
L = 8192
NBLK = 64
BATCH = 8


def pin_ends(rates, lowest, highest):
    flat = jnp.arange(C * MODES, dtype=jnp.int32).reshape(C, MODES)
    rates = jnp.where(flat == 0, lowest, rates)
    return jnp.where(flat == 1, highest, rates)


def draw_decay_rate(key, part):
    key = jax.random.fold_in(key, 11)
    lowest = 1.0 / (15.0 * L)
    highest = 1.0 / 4.0
    high = jnp.log(highest)
    low = jnp.log(lowest)
    return pin_ends(jnp.exp(jax.random.uniform(key, (C, MODES), jnp.float32, low, high)), lowest, highest)


def block_levels(own_key, shape, shards, smallest, top_value):
    factor_of, own = 1.0, jax.random.fold_in(own_key, 6)
    for dim, shards_of in shards:
        steps = jnp.exp(jax.random.uniform(jax.random.fold_in(own, dim), (shards_of,), jnp.float32, smallest / len(shards), top_value / len(shards)))
        factor_of = factor_of * jnp.repeat(steps, shape[dim] // shards_of).reshape([-1 if axis == dim else 1 for axis in range(len(shape))])
    return factor_of


def length_profile(count, total, most, slope):
    loads = [(1 << 20) // math.isqrt(rank ** slope) + 1 for rank in range(2, count + 1)]
    rest, holding = total - most - (count - 1), [1] * (count - 1)
    while rest > 0:
        candidates = [i for i in range(count - 1) if holding[i] < most]
        whole, left = sum([loads[i] for i in candidates]), rest
        for i in candidates:
            addition = min(most - holding[i], max(1, left * loads[i] // whole), rest)
            holding[i] = holding[i] + addition
            rest = rest - addition
    return np.array([most] + holding)


def uneven(rng, count, total, bound, lean):
    if count == 2:
        one = jax.random.randint(rng, (), max(1, total - bound), min(bound, total - 1) + 1)
        return jnp.stack([one, total - one])
    sizes = jnp.asarray(length_profile(count, total, bound, lean), jnp.int32)
    twos = (count - 1) // 2
    giver, receiver = sizes[1:1 + 2 * twos:2], sizes[2:2 + 2 * twos:2]
    margin = jnp.minimum(giver - 1, bound - receiver)
    shifted = jax.random.randint(jax.random.fold_in(rng, 1), (twos,), 0, 1 << 20) % (margin + 1)
    sizes = sizes.at[1:1 + 2 * twos:2].set(giver - shifted).at[2:2 + 2 * twos:2].set(receiver + shifted)
    return sizes[jax.random.permutation(jax.random.fold_in(rng, 2), count)]


def normal_values(key, extent, deviation, reach, shards=(), kind=jnp.bfloat16):
    values = jax.random.normal(key, extent, jnp.float32) * deviation
    if len(shards) > 0:
        values = block_levels(key, extent, shards, -0.22, 0.18) * values
    return jnp.clip(values, min=-reach, max=reach).astype(kind)


def setup_inputs(seed: int = 0) -> dict:
    streams_of = jax.random.split(jax.random.key(seed), 11)
    values = normal_values(streams_of[0], (BATCH, L, C), 1.0, 6.0, ((0, 8), (1, 16)))
    gate_one = normal_values(streams_of[1], (BATCH, L, C), 1.0, 6.0, ((0, 8), (1, 16)))
    gate_two = normal_values(streams_of[2], (BATCH, L, C), 1.0, 6.0, ((0, 8), (1, 16)))
    gate_three = normal_values(streams_of[3], (BATCH, L, C), 1.0, 6.0, ((0, 8), (1, 16)))
    genome_blocks = jax.vmap(lambda own: uneven(own, GENOMES, NBLK, NBLK // 2, 2))(jax.random.split(streams_of[4], BATCH)).reshape((BATCH, GENOMES)).astype(jnp.int32)
    short_taps = normal_values(streams_of[5], (SHORT_TAPS, C), SHORT_TAPS ** -0.5, 2.0)
    medium_taps = normal_values(streams_of[6], (MED_TAPS, C), MED_TAPS ** -0.5, 0.5, ((1, 8),))
    decay_rate = draw_decay_rate(jax.random.fold_in(streams_of[10], 71), 0)
    residue = normal_values(streams_of[8], (C, MODES), 0.25, 1.5, (), jnp.float32)
    long_skip = normal_values(streams_of[9], (C,), 0.3, 1.75, (), jnp.float32)
    return {"values": values, "gate_one": gate_one, "gate_two": gate_two, "gate_three": gate_three, "genome_blocks": genome_blocks, "short_taps": short_taps, "medium_taps": medium_taps, "decay_rate": decay_rate, "residue": residue, "long_skip": long_skip}


def block_flags(lengths, count):
    finish = jnp.cumsum(lengths)
    begin = finish - lengths
    block_ids = jnp.arange(count, dtype=jnp.int32)
    starts_here = jnp.any(block_ids[:, None] == begin[None, :], axis=1)
    return jnp.where(starts_here, 0.0, 1.0).astype(jnp.float32)

def causal_conv(signal, taps, keep):
    width = taps.shape[0]
    count = keep.shape[0]
    channels = signal.shape[1]
    grouped = signal.reshape(count, BLOCK, channels)
    opening = jnp.zeros((1, width - 1, channels), signal.dtype)
    tails = jnp.concatenate([opening, grouped[:-1, BLOCK - width + 1:]], axis=0)
    tails = tails * keep[:, None, None]
    windows = jnp.concatenate([tails, grouped], axis=1)
    length = 4 * BLOCK
    spectrum = jnp.fft.rfft(windows, n=length, axis=1) * jnp.fft.rfft(taps, n=length, axis=0)[None]
    result = jnp.fft.irfft(spectrum, n=length, axis=1)
    return result[:, width - 1:width - 1 + BLOCK].reshape(count * BLOCK, channels)

def reference(values, gate_one, gate_two, gate_three, genome_blocks, short_taps, medium_taps, decay_rate, residue, long_skip):
    amplitude = residue * jnp.sqrt(-jnp.expm1(-2.0 * decay_rate))
    index = jnp.arange(BLOCK).astype(jnp.float32)
    forward = jnp.exp(-index[:, None, None] * decay_rate[None])
    backward = jnp.exp(-(BLOCK - index)[:, None, None] * decay_rate[None])
    taps_long = jnp.einsum('icm,cm->ic', forward, amplitude, precision=lax.Precision.HIGHEST)
    block_decay = jnp.exp(-BLOCK * decay_rate)
    short_float = short_taps.astype(jnp.float32)
    medium_float = medium_taps.astype(jnp.float32)

    def advance(state, pair):
        factor_block, local_block = pair
        return (factor_block * state + local_block, state)

    def one_row(row):
        signal, first_gate, second_gate, third_gate, lengths = row
        keep = block_flags(lengths, NBLK)
        short_out = causal_conv(signal.astype(jnp.float32), short_float, keep)
        first = (first_gate * short_out).astype(jnp.bfloat16)
        medium_out = causal_conv(first.astype(jnp.float32), medium_float, keep)
        second = (second_gate * medium_out).astype(jnp.bfloat16)
        signal_two = second.astype(jnp.float32)
        intra = causal_conv(signal_two, taps_long, jnp.zeros((NBLK,), jnp.float32))
        grouped = signal_two.reshape(NBLK, BLOCK, C)
        local = jnp.einsum('bic,icm->bcm', grouped, backward, precision=lax.Precision.HIGHEST)
        factor = keep[:, None, None] * block_decay[None]
        start_state = jnp.zeros((C, MODES), jnp.float32)
        final_state, previous = lax.scan(advance, start_state, (factor, local))
        carried = keep[:, None, None] * previous * amplitude[None]
        carry = jnp.einsum('bcm,icm->bic', carried, forward, precision=lax.Precision.HIGHEST).reshape(L, C)
        long_out = intra + carry + long_skip[None] * signal_two
        return (third_gate * long_out).astype(jnp.bfloat16)
    return lax.map(one_row, (values, gate_one, gate_two, gate_three, genome_blocks))
```

```python
import functools

import jax
import jax.numpy as jnp
import numpy as np
from jax import lax
from jax.experimental import pallas as pl
from jax.experimental.pallas import tpu as pltpu
from jax.sharding import PartitionSpec as P

SHORT_TAPS = 7
MED_TAPS = 128
BLOCK = 128
WIDE = 256
MODES = 16
LANES = 128
F32 = jnp.float32
BF16 = jnp.bfloat16
VMEM_LIMIT = 56 * 1024 * 1024


def transform_matrices():
    n = np.arange(2 * BLOCK)
    j = np.arange(BLOCK)
    angle = np.pi * (2 * j + 1)[:, None] * n[None] / (2 * BLOCK)
    forward = np.concatenate([np.cos(angle), -np.sin(angle)], axis=0)
    backward = np.concatenate([np.cos(angle).T, -np.sin(angle).T], axis=1) / BLOCK
    high = forward.astype(jnp.bfloat16)
    low = (forward - high.astype(np.float64)).astype(jnp.bfloat16)
    return high, low[:, :BLOCK], backward[BLOCK:].astype(jnp.bfloat16), backward[:BLOCK].astype(jnp.bfloat16)


def keep_scalars(genome_ref, position, count):
    begins = [jnp.int32(0)]
    for g in range(genome_ref.shape[1] - 1):
        begins.append(begins[-1] + genome_ref[0, g])
    keeps = []
    for b in range(count):
        block = position * count + b
        starts = functools.reduce(jnp.logical_or, [block == begin for begin in begins])
        keeps.append(jnp.where(starts, 0.0, 1.0).astype(F32))
    return keeps


def dot(a, b):
    return jnp.dot(a, b, preferred_element_type=F32)


def spectral_product(spec, taps_spec):
    wr, wi = spec[:BLOCK], spec[BLOCK:]
    tr, ti = taps_spec[:BLOCK], taps_spec[BLOCK:]
    return jnp.concatenate([(wr * tr - wi * ti).astype(BF16), (wr * ti + wi * tr).astype(BF16)], axis=0)


def kernel_first(genome_ref, values_ref, rim_ref, gate_ref, taps_ref, first_ref, window):
    count = values_ref.shape[0] // BLOCK
    keeps = keep_scalars(genome_ref, lax.axis_index("seq"), count)
    taps = taps_ref[...].astype(F32)
    for b in range(count):
        start = b * BLOCK
        for tile in range(WIDE // LANES):
            lanes = slice(tile * LANES, (tile + 1) * LANES)
            before = rim_ref[:, lanes] if b == 0 else values_ref[start - 16 : start, lanes]
            slot = b * (WIDE // LANES) + tile
            window[slot, 0:16] = before.astype(F32) * keeps[b]
            window[slot, 16 : 16 + BLOCK] = values_ref[start : start + BLOCK, lanes].astype(F32)
            total = window[slot, 16 : 16 + BLOCK] * taps[0:1, lanes]
            for k in range(1, SHORT_TAPS):
                total = total + window[slot, 16 - k : 16 - k + BLOCK] * taps[k : k + 1, lanes]
            gated = gate_ref[start : start + BLOCK, lanes].astype(F32) * total
            first_ref[start : start + BLOCK, lanes] = gated.astype(BF16)


def kernel_second(
    genome_ref, first_ref, halo_ref, gate_ref, taps_ref, rate_ref, fwd_ref, low_ref, back_ref, second_ref, local_ref
):
    count = first_ref.shape[0] // BLOCK
    keeps = keep_scalars(genome_ref, lax.axis_index("seq"), count)
    taps = taps_ref[...]
    taps_spec = dot(fwd_ref[:, :BLOCK], taps) + dot(low_ref[...], taps)
    for b in range(count):
        start = b * BLOCK
        before = halo_ref[...] if b == 0 else first_ref[start - BLOCK : start]
        spec = dot(fwd_ref[:, BLOCK:], first_ref[start : start + BLOCK]) + dot(fwd_ref[:, :BLOCK], before) * keeps[b]
        medium = dot(back_ref[...], spectral_product(spec, taps_spec))
        second_ref[start : start + BLOCK] = (gate_ref[start : start + BLOCK].astype(F32) * medium).astype(BF16)
    sub = lax.broadcasted_iota(jnp.int32, (1, 8, 1), 1).astype(F32)
    for tile in range(WIDE // LANES):
        lanes = slice(tile * LANES, (tile + 1) * LANES)
        rate = rate_ref[:, lanes][:, None, :]
        step = jnp.broadcast_to(jnp.exp(-8.0 * rate), (MODES, 8, LANES))
        weight = jnp.exp((sub - 8.0) * rate)
        for b in range(count):
            signal = second_ref[b * BLOCK : (b + 1) * BLOCK, lanes].astype(F32)
            acc = jnp.broadcast_to(signal[0:8][None], (MODES, 8, LANES))
            for j in range(1, BLOCK // 8):
                acc = acc * step + signal[8 * j : 8 * j + 8][None]
            local_ref[b, :, lanes] = jnp.sum(acc * weight, axis=1)


def kernel_mixed(
    genome_ref, second_ref, gate_ref, local_ref, incoming_ref, rate_ref, amplitude_ref, skip_ref, fwd_ref, low_ref, back_ref,
    mixed_ref, filt, carry,
):
    count = second_ref.shape[0] // BLOCK
    keeps = keep_scalars(genome_ref, lax.axis_index("seq"), count)
    sub = lax.broadcasted_iota(jnp.int32, (1, 8, 1), 1).astype(F32)
    for tile in range(WIDE // LANES):
        lanes = slice(tile * LANES, (tile + 1) * LANES)
        rate = rate_ref[:, lanes]
        amplitude = amplitude_ref[:, lanes]
        decay = jnp.exp(-float(BLOCK) * rate)
        rate = rate[:, None, :]
        step = jnp.broadcast_to(jnp.exp(-8.0 * rate), (MODES, 8, LANES))
        weight = amplitude[:, None, :] * jnp.exp(-sub * rate)
        part = weight
        for j in range(BLOCK // 8):
            filt[8 * j : 8 * j + 8, lanes] = jnp.sum(part, axis=0)
            part = part * step
        filt[0:1, lanes] = filt[0:1, lanes] + skip_ref[0:1, lanes]
        state = incoming_ref[:, lanes]
        for b in range(count):
            state = state * keeps[b]
            part = weight * state[:, None, :]
            for j in range(BLOCK // 8):
                carry[b * BLOCK + 8 * j : b * BLOCK + 8 * j + 8, lanes] = jnp.sum(part, axis=0)
                part = part * step
            if b < count - 1:
                state = decay * state + local_ref[b, :, lanes]
    taps = filt[...]
    high = taps.astype(BF16)
    low = (taps - high.astype(F32)).astype(BF16)
    taps_spec = dot(fwd_ref[:, :BLOCK], high) + dot(low_ref[...], high) + dot(fwd_ref[:, :BLOCK], low)
    for b in range(count):
        rows = slice(b * BLOCK, (b + 1) * BLOCK)
        spec = dot(fwd_ref[:, :BLOCK], second_ref[rows])
        total = dot(back_ref[...], spectral_product(spec, taps_spec)) + carry[rows]
        mixed_ref[rows] = (gate_ref[rows].astype(F32) * total).astype(BF16)


def chunked(rows):
    return pl.BlockSpec((rows, WIDE), lambda i: (0, i))


def whole(shape):
    return pl.BlockSpec(shape, lambda i: (0,) * len(shape))


def scan_states(total, rate, genome, parts, count):
    begin = jnp.cumsum(genome) - genome
    blocks = jnp.arange(parts * count, dtype=jnp.int32)
    keep = jnp.where(jnp.any(blocks[:, None] == begin[None], axis=1), 0.0, 1.0).astype(F32)
    through = jnp.prod(keep.reshape(parts, count), axis=1)
    decay = jnp.exp(-float(count * BLOCK) * rate)
    state = jnp.zeros_like(total[0])
    incoming = []
    for p in range(parts):
        incoming.append(state)
        state = through[p] * decay * state + total[p]
    return jnp.stack(incoming)


def body(values, gate_one, gate_two, gate_three, genome_blocks, short_taps, medium_taps, decay_rate, residue, long_skip):
    medium_full = lax.all_gather(medium_taps, "dp", axis=1, tiled=True)
    rows, channels = values.shape[1:]
    count = rows // BLOCK
    parts = lax.axis_size("seq")
    position = lax.axis_index("seq")
    pairs = [(i, i + 1) for i in range(parts - 1)]
    fwd, low, back_end, back_start = [jnp.asarray(m) for m in transform_matrices()]
    rate = decay_rate.T
    amplitude = residue.T * jnp.sqrt(-jnp.expm1(-2.0 * rate))
    signal = values[0]
    grid = (channels // WIDE,)
    params = pltpu.CompilerParams(vmem_limit_bytes=VMEM_LIMIT)
    smem = pl.BlockSpec(memory_space=pltpu.SMEM)

    rim = lax.ppermute(signal[rows - 16 :], "seq", pairs)
    first = pl.pallas_call(
        kernel_first,
        grid=grid,
        in_specs=[smem, chunked(rows), chunked(16), chunked(rows), chunked(SHORT_TAPS)],
        out_specs=chunked(rows),
        out_shape=jax.ShapeDtypeStruct((rows, channels), BF16),
        scratch_shapes=[pltpu.VMEM((count * (WIDE // LANES), 16 + BLOCK, LANES), F32)],
        compiler_params=params,
        name="first",
    )(genome_blocks, signal, rim, gate_one[0], short_taps)
    halo = lax.ppermute(first[rows - BLOCK :], "seq", pairs)
    second, local = pl.pallas_call(
        kernel_second,
        grid=grid,
        in_specs=[
            smem, chunked(rows), chunked(BLOCK), chunked(rows), chunked(BLOCK), chunked(MODES),
            whole(fwd.shape), whole(low.shape), whole(back_end.shape),
        ],
        out_specs=[chunked(rows), pl.BlockSpec((count, MODES, WIDE), lambda i: (0, 0, i))],
        out_shape=[
            jax.ShapeDtypeStruct((rows, channels), BF16),
            jax.ShapeDtypeStruct((count, MODES, channels), F32),
        ],
        compiler_params=params,
        name="second",
    )(genome_blocks, first, halo, gate_two[0], medium_full, rate, fwd, low, back_end)

    begin = jnp.cumsum(genome_blocks[0]) - genome_blocks[0]
    blocks = position * count + jnp.arange(count, dtype=jnp.int32)
    keep = jnp.where(jnp.any(blocks[:, None] == begin[None], axis=1), 0.0, 1.0).astype(F32)
    decay = jnp.exp(-float(BLOCK) * rate)
    total = local[0]
    for b in range(1, count):
        total = keep[b] * decay * total + local[b]
    width = channels // parts
    ends = lax.all_to_all(total.reshape(MODES, parts, width), "seq", split_axis=1, concat_axis=0, tiled=False)
    rate_part = lax.dynamic_slice_in_dim(rate, position * width, width, 1)
    incoming = scan_states(ends, rate_part, genome_blocks[0], parts, count)
    incoming = lax.all_to_all(incoming, "seq", split_axis=0, concat_axis=1, tiled=False).reshape(MODES, channels)

    mixed = pl.pallas_call(
        kernel_mixed,
        grid=grid,
        in_specs=[
            smem, chunked(rows), chunked(rows), pl.BlockSpec((count, MODES, WIDE), lambda i: (0, 0, i)),
            chunked(MODES), chunked(MODES), chunked(MODES), chunked(1),
            whole(fwd.shape), whole(low.shape), whole(back_start.shape),
        ],
        out_specs=chunked(rows),
        out_shape=jax.ShapeDtypeStruct((rows, channels), BF16),
        scratch_shapes=[pltpu.VMEM((BLOCK, WIDE), F32), pltpu.VMEM((rows, WIDE), F32)],
        compiler_params=params,
        name="mixed",
    )(
        genome_blocks, second, gate_three[0], local, incoming, rate, amplitude, long_skip[None],
        fwd, low, back_start,
    )
    return mixed[None]


def solution(mesh):
    return jax.shard_map(
        body,
        mesh=mesh,
        in_specs=(
            P("dp", "seq", None),
            P("dp", "seq", None),
            P("dp", "seq", None),
            P("dp", "seq", None),
            P("dp", None),
            P(),
            P(None, "dp"),
            P(),
            P(),
            P(),
        ),
        out_specs=P("dp", "seq", None),
        check_vma=False,
    )
```

```python
import functools

import jax
import jax.numpy as jnp
import numpy as np
from jax import lax
from jax.experimental import pallas as pl
from jax.experimental.pallas import tpu as pltpu
from jax.sharding import PartitionSpec as P

SHORT_TAPS = 7
MED_TAPS = 128
BLOCK = 128
WIDE = 512
MODES = 16
LANES = 128
F32 = jnp.float32
BF16 = jnp.bfloat16
VMEM_LIMIT = 58 * 1024 * 1024


def transform_matrices():
    n = np.arange(2 * BLOCK)
    j = np.arange(BLOCK)
    angle = np.pi * (2 * j + 1)[:, None] * n[None] / (2 * BLOCK)
    forward = np.concatenate([np.cos(angle), -np.sin(angle)], axis=0)
    backward = np.concatenate([np.cos(angle).T, -np.sin(angle).T], axis=1) / BLOCK
    high = forward.astype(jnp.bfloat16)
    low = (forward - high.astype(np.float64)).astype(jnp.bfloat16)
    return high, low[:, :BLOCK], backward[BLOCK:].astype(jnp.bfloat16), backward[:BLOCK].astype(jnp.bfloat16)


def keep_scalars(genome_ref, position, count):
    begins = [jnp.int32(0)]
    for g in range(genome_ref.shape[1] - 1):
        begins.append(begins[-1] + genome_ref[0, g])
    keeps = []
    for b in range(count):
        block = position * count + b
        starts = functools.reduce(jnp.logical_or, [block == begin for begin in begins])
        keeps.append(jnp.where(starts, 0.0, 1.0).astype(F32))
    return keeps


def dot(a, b):
    return jnp.dot(a, b, preferred_element_type=F32)


def staged(fwd_of, signal_of, back, taps_spec, spec, product, blocks):
    for b in blocks:
        spec[b] = dot(fwd_of(b), signal_of(b))
    for b in blocks:
        for r in range(0, BLOCK, 16):
            re, im = slice(r, r + 16), slice(BLOCK + r, BLOCK + r + 16)
            wr, wi, tr, ti = spec[b, re], spec[b, im], taps_spec(re), taps_spec(im)
            product[b, re] = (wr * tr - wi * ti).astype(BF16)
            product[b, im] = (wr * ti + wi * tr).astype(BF16)
    return [(b, dot(back, product[b])) for b in blocks]


def lane_window(i, width):
    return pl.ds(pl.multiple_of(i * width, width), width)


def short_block(values, before, gate, taps, keep, window, first, rows, i):
    for tile in range(WIDE // LANES):
        lanes = pl.ds(pl.multiple_of(i * WIDE + tile * LANES, LANES), LANES)
        window[tile, 0:16] = before(lanes).astype(F32) * keep
        window[tile, 16 : 16 + BLOCK] = values[rows, lanes].astype(F32)
        weights = taps[:, lanes].astype(F32)
        total = window[tile, 16 : 16 + BLOCK] * weights[0:1]
        for k in range(1, SHORT_TAPS):
            total = total + window[tile, 16 - k : 16 - k + BLOCK] * weights[k : k + 1]
        first[rows, lanes] = (gate[rows, lanes].astype(F32) * total).astype(BF16)


def block_states(second, rate_ref, local, blocks, i):
    sub = lax.broadcasted_iota(jnp.int32, (1, 8, 1), 1).astype(F32)
    for tile in range(WIDE // LANES):
        lanes = pl.ds(pl.multiple_of(i * WIDE + tile * LANES, LANES), LANES)
        rate = rate_ref[:, lanes][:, None, :]
        step = jnp.broadcast_to(jnp.exp(-8.0 * rate), (MODES, 8, LANES))
        weight = jnp.exp((sub - 8.0) * rate)
        for b in blocks:
            signal = second[b * BLOCK : (b + 1) * BLOCK, lanes].astype(F32)
            acc = jnp.broadcast_to(signal[0:8][None], (MODES, 8, LANES))
            for j in range(1, BLOCK // 8):
                acc = acc * step + signal[8 * j : 8 * j + 8][None]
            local[b, :, lanes] = jnp.sum(acc * weight, axis=1)


def kernel_states(
    genome_ref, values_hbm, gate_one_hbm, gate_two_hbm, short_ref, taps_ref, rate_ref, fwd_ref, low_ref, back_ref,
    second_out, local_out, incoming_out,
    values, gate_one, gate_two, first, second, halo, rim, taps_full, taps_spec, local, ends_own, ends, entering,
    fwd_keep, window, spec, product,
    load_sem, store_sem, rim_sem, halo_send, halo_recv, taps_send, taps_recv, ends_send, ends_recv, enter_send, enter_recv,
):
    rows, channels = values.shape
    count = rows // BLOCK
    chunks = channels // WIDE
    parts = lax.axis_size("seq")
    width = channels // parts
    per_chunk = WIDE // width
    dps = lax.axis_size("dp")
    chips = dps // 2
    seq = lax.axis_index("seq")
    dp = lax.axis_index("dp")
    chip, core = dp // 2, dp % 2
    twin = chip * 2 + (1 - core)
    following = lax.rem(seq + 1, parts)
    keeps = keep_scalars(genome_ref, seq, count)
    tail = rows - BLOCK

    def remote(src, dst, send, recv, dp_to, seq_to):
        return pltpu.make_async_remote_copy(
            src_ref=src, dst_ref=dst, send_sem=send, recv_sem=recv,
            device_id=(dp_to, seq_to), device_id_type=pl.DeviceIdType.MESH,
        )

    loads = []
    for src, dst, part in (
        (values_hbm, values, slice(tail - 16, rows)),
        (gate_one_hbm, gate_one, slice(tail, rows)),
        (values_hbm, values, slice(0, tail - 16)),
        (gate_one_hbm, gate_one, slice(0, tail)),
        (gate_two_hbm, gate_two, slice(0, rows)),
    ):
        copy = pltpu.make_async_copy(src.at[part], dst.at[part], load_sem.at[len(loads)])
        copy.start()
        loads.append(copy)

    barrier = pltpu.get_barrier_semaphore()
    peers = 0
    for k in range(1, parts):
        pl.semaphore_signal(
            barrier, inc=1, device_id=(dp, lax.rem(seq + k, parts)), device_id_type=pl.DeviceIdType.MESH
        )
        peers += 1
    for k in range(1, chips):
        pl.semaphore_signal(
            barrier, inc=1, device_id=(lax.rem(chip + k, chips) * 2 + core, seq), device_id_type=pl.DeviceIdType.MESH
        )
        peers += 1
    pl.semaphore_signal(barrier, inc=1, device_id=(twin, seq), device_id_type=pl.DeviceIdType.MESH)
    pl.semaphore_wait(barrier, peers + 1)

    rim_copy = remote(values_hbm.at[slice(rows - 16, rows)], rim, rim_sem.at[0], rim_sem.at[1], dp, following)
    rim_copy.start()

    def taps_copy(slot, index, src, dp_to):
        return remote(src, taps_full.at[slot], taps_send.at[index], taps_recv.at[slot], dp_to, seq)

    taps_own = pltpu.make_async_copy(taps_ref, taps_full.at[dp], taps_recv.at[dp])
    taps_own.start()
    taps_copies = [taps_copy(dp, k - 1, taps_ref, lax.rem(chip + k, chips) * 2 + core) for k in range(1, chips)]
    taps_copies.append(taps_copy(dp, chips - 1, taps_ref, twin))
    for copy in taps_copies:
        copy.start()

    loads[0].wait()
    loads[1].wait()

    def halo_copy(i):
        lanes = lane_window(i, WIDE)
        return remote(
            first.at[slice(tail, rows), lanes], halo.at[:, lanes], halo_send.at[i], halo_recv.at[i], dp, following
        )

    def tail_step(i, carry):
        short_block(
            values, lambda lanes: values[tail - 16 : tail, lanes], gate_one, short_ref, keeps[count - 1], window, first,
            slice(tail, rows), i,
        )
        halo_copy(i).start()
        return carry

    lax.fori_loop(0, chunks, tail_step, 0)

    for b in range(count):
        column = lax.broadcasted_iota(jnp.int32, fwd_ref.shape, 1)
        matrix = fwd_ref[...].astype(F32)
        fwd_keep[b] = jnp.where(column < BLOCK, matrix * keeps[b], matrix).astype(BF16)

    loads[2].wait()
    loads[3].wait()
    rim_copy.wait()

    def first_step(i, carry):
        for b in range(count - 1):
            start = b * BLOCK
            if b == 0:
                before = lambda lanes: rim[:, lanes]
            else:
                before = lambda lanes, start=start: values[start - 16 : start, lanes]
            short_block(values, before, gate_one, short_ref, keeps[b], window, first, slice(start, start + BLOCK), i)
        return carry

    lax.fori_loop(0, chunks, first_step, 0)

    forwards = []
    for k in range(1, chips):
        source = lax.rem(chip + k, chips) * 2 + core
        taps_copy(source, k - 1, taps_ref, source).wait_recv()
        copy = taps_copy(source, chips - 1 + k, taps_full.at[source], twin)
        copy.start()
        forwards.append(copy)
    taps_own.wait()
    for k in range(chips):
        source = lax.rem(chip + k, chips) * 2 + (1 - core)
        taps_copy(source, chips - 1, taps_ref, twin).wait_recv()
    loads[4].wait()

    def second_step(i, carry):
        lanes = lane_window(i, WIDE)
        taps = taps_full[i]
        taps_spec[:, lanes] = dot(fwd_ref[:, :BLOCK], taps) + dot(low_ref[...], taps)
        blocks = range(1, count)
        for b, medium in staged(
            lambda b: fwd_keep[b], lambda b: first[(b - 1) * BLOCK : (b + 1) * BLOCK, lanes], back_ref[...],
            lambda part: taps_spec[part, lanes], spec, product, blocks,
        ):
            part = slice(b * BLOCK, (b + 1) * BLOCK)
            second[part, lanes] = (gate_two[part, lanes].astype(F32) * medium).astype(BF16)
        block_states(second, rate_ref, local, blocks, i)
        return carry

    lax.fori_loop(0, chunks, second_step, 0)
    late = slice(BLOCK, rows)
    store_late = pltpu.make_async_copy(second.at[late], second_out.at[late], store_sem.at[0])
    store_late.start()

    def ends_copy(part):
        return remote(ends_own.at[part], ends.at[seq], ends_send.at[part], ends_recv.at[seq], dp, part)

    def opening_step(i, carry):
        lanes = lane_window(i, WIDE)
        halo_copy(i).wait_recv()
        spec[0] = dot(fwd_keep[0, :, :BLOCK], halo[:, lanes]) + dot(fwd_keep[0, :, BLOCK:], first[0:BLOCK, lanes])
        for r in range(0, BLOCK, 16):
            re, im = slice(r, r + 16), slice(BLOCK + r, BLOCK + r + 16)
            wr, wi, tr, ti = spec[0, re], spec[0, im], taps_spec[re, lanes], taps_spec[im, lanes]
            product[0, re] = (wr * tr - wi * ti).astype(BF16)
            product[0, im] = (wr * ti + wi * tr).astype(BF16)
        medium = dot(back_ref[...], product[0])
        second[0:BLOCK, lanes] = (gate_two[0:BLOCK, lanes].astype(F32) * medium).astype(BF16)
        block_states(second, rate_ref, local, range(1), i)
        decay = jnp.exp(-float(BLOCK) * rate_ref[:, lanes])
        total = local[0, :, lanes]
        for b in range(1, count):
            total = keeps[b] * decay * total + local[b, :, lanes]
        for h in range(per_chunk):
            part = i * per_chunk + h
            ends_own[part] = total[:, h * width : (h + 1) * width]

            @pl.when(part != seq)
            def _():
                ends_copy(part).start()

            @pl.when(part == seq)
            def _():
                ends[part] = total[:, h * width : (h + 1) * width]

        return carry

    lax.fori_loop(0, chunks, opening_step, 0)
    early = slice(0, BLOCK)
    store_early = pltpu.make_async_copy(second.at[early], second_out.at[early], store_sem.at[1])
    store_early.start()
    store_local = pltpu.make_async_copy(local, local_out, store_sem.at[2])
    store_local.start()

    def arrival(k, carry):
        source = lax.rem(seq + k, parts)
        remote(ends_own.at[source], ends.at[source], ends_send.at[source], ends_recv.at[source], dp, source).wait_recv()
        return carry

    lax.fori_loop(1, parts, arrival, 0)

    begins = [jnp.int32(0)]
    for g in range(genome_ref.shape[1] - 1):
        begins.append(begins[-1] + genome_ref[0, g])
    decay = jnp.exp(-float(rows) * rate_ref[:, lane_window(seq, width)])

    def enter_copy(p):
        return remote(entering.at[p], incoming_out.at[seq], enter_send.at[p], enter_recv.at[seq], dp, p)

    def scan_step(p, state):
        entering[p] = state

        @pl.when(p != seq)
        def _():
            enter_copy(p).start()

        through = jnp.float32(1.0)
        for b in range(count):
            for begin in begins:
                through = jnp.where(p * count + b == begin, 0.0, through)
        return through * decay * state + ends[p]

    lax.fori_loop(0, parts, scan_step, jnp.zeros((MODES, width), F32))
    enter_own = pltpu.make_async_copy(entering.at[seq], incoming_out.at[seq], store_sem.at[3])
    enter_own.start()

    def departures(k, carry):
        other = lax.rem(seq + k, parts)
        ends_copy(other).wait_send()
        enter_copy(other).wait_send()
        remote(entering.at[other], incoming_out.at[other], enter_send.at[other], enter_recv.at[other], dp, other).wait_recv()
        return carry

    lax.fori_loop(1, parts, departures, 0)

    def halo_sent(i, carry):
        halo_copy(i).wait_send()
        return carry

    lax.fori_loop(0, chunks, halo_sent, 0)
    for copy in taps_copies + forwards:
        copy.wait_send()
    for copy in (store_late, store_early, store_local, enter_own):
        copy.wait()


def kernel_mixed(
    genome_ref, second_ref, gate_ref, local_ref, incoming_ref, rate_ref, amplitude_ref, skip_ref, fwd_ref, low_ref, back_ref,
    mixed_ref, filt, carry, taps_spec, spec, product,
):
    count = second_ref.shape[0] // BLOCK
    keeps = keep_scalars(genome_ref, lax.axis_index("seq"), count)
    sub = lax.broadcasted_iota(jnp.int32, (1, 8, 1), 1).astype(F32)
    pieces, _, width = incoming_ref.shape
    for tile in range(WIDE // LANES):
        lanes = slice(tile * LANES, (tile + 1) * LANES)
        rate = rate_ref[:, lanes]
        decay = jnp.exp(-float(BLOCK) * rate)
        rate = rate[:, None, :]
        step = jnp.broadcast_to(jnp.exp(-8.0 * rate), (MODES, 8, LANES))
        weight = amplitude_ref[:, lanes][:, None, :] * jnp.exp(-sub * rate)
        part = weight
        for j in range(BLOCK // 8):
            filt[8 * j : 8 * j + 8, lanes] = jnp.sum(part, axis=0)
            part = part * step
        filt[0:1, lanes] = filt[0:1, lanes] + skip_ref[0:1, lanes]
    taps = filt[...]
    high = taps.astype(BF16)
    low = (taps - high.astype(F32)).astype(BF16)
    taps_spec[...] = dot(fwd_ref[:, :BLOCK], high) + dot(low_ref[...], high) + dot(fwd_ref[:, :BLOCK], low)
    for b in range(count):
        spec[b] = dot(fwd_ref[:, :BLOCK], second_ref[b * BLOCK : (b + 1) * BLOCK])
    for tile in range(WIDE // LANES):
        lanes = slice(tile * LANES, (tile + 1) * LANES)
        rate = rate_ref[:, lanes]
        decay = jnp.exp(-float(BLOCK) * rate)
        rate = rate[:, None, :]
        step = jnp.broadcast_to(jnp.exp(-8.0 * rate), (MODES, 8, LANES))
        weight = amplitude_ref[:, lanes][:, None, :] * jnp.exp(-sub * rate)
        piece, offset = tile * LANES // width, tile * LANES % width
        state = incoming_ref[piece, :, offset : offset + LANES]
        for b in range(count):
            state = state * keeps[b]
            part = weight * state[:, None, :]
            for j in range(BLOCK // 8):
                carry[b * BLOCK + 8 * j : b * BLOCK + 8 * j + 8, lanes] = jnp.sum(part, axis=0)
                part = part * step
            if b < count - 1:
                state = decay * state + local_ref[b, :, lanes]
    for b in range(count):
        for r in range(0, BLOCK, 16):
            re, im = slice(r, r + 16), slice(BLOCK + r, BLOCK + r + 16)
            wr, wi, tr, ti = spec[b, re], spec[b, im], taps_spec[re], taps_spec[im]
            product[b, re] = (wr * tr - wi * ti).astype(BF16)
            product[b, im] = (wr * ti + wi * tr).astype(BF16)
    for b in range(count):
        rows = slice(b * BLOCK, (b + 1) * BLOCK)
        total = dot(back_ref[...], product[b]) + carry[rows]
        mixed_ref[rows] = (gate_ref[rows].astype(F32) * total).astype(BF16)


def chunked(rows):
    return pl.BlockSpec((rows, WIDE), lambda i: (0, i))


def whole(shape):
    return pl.BlockSpec(shape, lambda i: (0,) * len(shape))


def body(values, gate_one, gate_two, gate_three, genome_blocks, short_taps, medium_taps, decay_rate, residue, long_skip):
    rows, channels = values.shape[1:]
    count = rows // BLOCK
    parts = lax.axis_size("seq")
    dps = lax.axis_size("dp")
    width = channels // parts
    chunks = channels // WIDE
    fwd, low, back_end, back_start = [jnp.asarray(m) for m in transform_matrices()]
    rate = decay_rate.T
    amplitude = residue.T * jnp.sqrt(-jnp.expm1(-2.0 * rate))
    smem = pl.BlockSpec(memory_space=pltpu.SMEM)
    vmem = pl.BlockSpec(memory_space=pltpu.VMEM)
    hbm = pl.BlockSpec(memory_space=pl.ANY)
    stream = pltpu.VMEM((rows, channels), BF16)
    dma = pltpu.SemaphoreType.DMA

    second, local, incoming = pl.pallas_call(
        kernel_states,
        in_specs=[smem, hbm, hbm, hbm, vmem, vmem, vmem, vmem, vmem, vmem],
        out_specs=[hbm, hbm, hbm],
        out_shape=[
            jax.ShapeDtypeStruct((rows, channels), BF16),
            jax.ShapeDtypeStruct((count, MODES, channels), F32),
            jax.ShapeDtypeStruct((parts, MODES, width), F32),
        ],
        scratch_shapes=[
            stream, stream, stream, stream, stream,
            pltpu.VMEM((BLOCK, channels), BF16),
            pltpu.VMEM((16, channels), BF16),
            pltpu.VMEM((dps, BLOCK, WIDE), BF16),
            pltpu.VMEM((2 * BLOCK, channels), F32),
            pltpu.VMEM((count, MODES, channels), F32),
            pltpu.VMEM((parts, MODES, width), F32),
            pltpu.VMEM((parts, MODES, width), F32),
            pltpu.VMEM((parts, MODES, width), F32),
            pltpu.VMEM((count, 2 * BLOCK, 2 * BLOCK), BF16),
            pltpu.VMEM((WIDE // LANES, 16 + BLOCK, LANES), F32),
            pltpu.VMEM((count, 2 * BLOCK, WIDE), F32),
            pltpu.VMEM((count, 2 * BLOCK, WIDE), BF16),
            dma((5,)), dma((4,)), dma((2,)), dma((chunks,)), dma((chunks,)), dma((dps,)), dma((dps,)),
            dma((parts,)), dma((parts,)), dma((parts,)), dma((parts,)),
        ],
        compiler_params=pltpu.CompilerParams(
            vmem_limit_bytes=VMEM_LIMIT, collective_id=0, has_side_effects=True
        ),
        name="states",
    )(genome_blocks, values[0], gate_one[0], gate_two[0], short_taps, medium_taps, rate, fwd, low, back_end)

    per_chunk = WIDE // width
    mixed = pl.pallas_call(
        kernel_mixed,
        grid=(chunks,),
        in_specs=[
            smem, chunked(rows), chunked(rows), pl.BlockSpec((count, MODES, WIDE), lambda i: (0, 0, i)),
            pl.BlockSpec((per_chunk, MODES, width), lambda i: (i, 0, 0)),
            chunked(MODES), chunked(MODES), chunked(1),
            whole(fwd.shape), whole(low.shape), whole(back_start.shape),
        ],
        out_specs=chunked(rows),
        out_shape=jax.ShapeDtypeStruct((rows, channels), BF16),
        scratch_shapes=[
            pltpu.VMEM((BLOCK, WIDE), F32),
            pltpu.VMEM((rows, WIDE), F32),
            pltpu.VMEM((2 * BLOCK, WIDE), F32),
            pltpu.VMEM((count, 2 * BLOCK, WIDE), F32),
            pltpu.VMEM((count, 2 * BLOCK, WIDE), BF16),
        ],
        compiler_params=pltpu.CompilerParams(vmem_limit_bytes=VMEM_LIMIT),
        name="mixed",
    )(genome_blocks, second, gate_three[0], local, incoming, rate, amplitude, long_skip[None], fwd, low, back_start)
    return mixed[None]


def solution(mesh):
    return jax.shard_map(
        body,
        mesh=mesh,
        in_specs=(
            P("dp", "seq", None),
            P("dp", "seq", None),
            P("dp", "seq", None),
            P("dp", "seq", None),
            P("dp", None),
            P(),
            P(None, "dp"),
            P(),
            P(),
            P(),
        ),
        out_specs=P("dp", "seq", None),
        check_vma=False,
    )
```

```python
import functools

import jax
import jax.numpy as jnp
import numpy as np
from jax import lax
from jax.experimental import pallas as pl
from jax.experimental.pallas import tpu as pltpu
from jax.sharding import PartitionSpec as P

SHORT_TAPS = 7
MED_TAPS = 128
BLOCK = 128
WIDE = 512
MODES = 16
LANES = 128
F32 = jnp.float32
BF16 = jnp.bfloat16
INTRA = F32
VMEM_LIMIT = 58 * 1024 * 1024


def transform_matrices():
    n = np.arange(2 * BLOCK)
    j = np.arange(BLOCK)
    angle = np.pi * (2 * j + 1)[:, None] * n[None] / (2 * BLOCK)
    forward = np.concatenate([np.cos(angle), -np.sin(angle)], axis=0)
    backward = np.concatenate([np.cos(angle).T, -np.sin(angle).T], axis=1) / BLOCK
    high = forward.astype(jnp.bfloat16)
    low = (forward - high.astype(np.float64)).astype(jnp.bfloat16)
    return high, low[:, :BLOCK], backward[BLOCK:].astype(jnp.bfloat16), backward[:BLOCK].astype(jnp.bfloat16)


def keep_scalars(genome_ref, position, count):
    begins = [jnp.int32(0)]
    for g in range(genome_ref.shape[1] - 1):
        begins.append(begins[-1] + genome_ref[0, g])
    keeps = []
    for b in range(count):
        block = position * count + b
        starts = functools.reduce(jnp.logical_or, [block == begin for begin in begins])
        keeps.append(jnp.where(starts, 0.0, 1.0).astype(F32))
    return keeps


def dot(a, b):
    return jnp.dot(a, b, preferred_element_type=F32)


def pointwise(spec, product, taps_spec, b):
    for r in range(0, BLOCK, 16):
        re, im = slice(r, r + 16), slice(BLOCK + r, BLOCK + r + 16)
        wr, wi, tr, ti = spec[b, re], spec[b, im], taps_spec(re), taps_spec(im)
        product[b, re] = (wr * tr - wi * ti).astype(BF16)
        product[b, im] = (wr * ti + wi * tr).astype(BF16)


def staged(fwd_of, signal_of, back, taps_spec, spec, product, blocks):
    for b in blocks:
        spec[b] = dot(fwd_of(b), signal_of(b))
    for b in blocks:
        pointwise(spec, product, taps_spec, b)
    return [(b, dot(back, product[b])) for b in blocks]


def lane_window(i, width):
    return pl.ds(pl.multiple_of(i * width, width), width)


def short_block(values, before, gate, taps, keep, window, first, rows, i):
    for tile in range(WIDE // LANES):
        lanes = pl.ds(pl.multiple_of(i * WIDE + tile * LANES, LANES), LANES)
        window[tile, 0:16] = before(lanes).astype(F32) * keep
        window[tile, 16 : 16 + BLOCK] = values[rows, lanes].astype(F32)
        weights = taps[:, lanes].astype(F32)
        total = window[tile, 16 : 16 + BLOCK] * weights[0:1]
        for k in range(1, SHORT_TAPS):
            total = total + window[tile, 16 - k : 16 - k + BLOCK] * weights[k : k + 1]
        first[rows, lanes] = (gate[rows, lanes].astype(F32) * total).astype(BF16)


def sublane_sums(stack):
    sub = lax.broadcasted_iota(jnp.int32, (8, LANES), 0)
    groups = []
    for g in range(0, MODES, 8):
        level = [stack[g + m] for m in range(8)]
        for shift in (1, 2, 4):
            low = (sub & shift) == 0
            level = [
                jnp.where(low, a, b) + pltpu.roll(jnp.where(low, b, a), shift, 0)
                for a, b in zip(level[0::2], level[1::2])
            ]
        groups.append(level[0])
    return jnp.concatenate(groups, axis=0)


def long_filter(rate_ref, residue_ref, skip_ref, fwd_ref, low_ref, amplitude_ref, filt, long_spec, i):
    sub = lax.broadcasted_iota(jnp.int32, (1, 8, 1), 1).astype(F32)
    for tile in range(WIDE // LANES):
        own = slice(tile * LANES, (tile + 1) * LANES)
        lanes = pl.ds(pl.multiple_of(i * WIDE + tile * LANES, LANES), LANES)
        rate = rate_ref[:, lanes]
        x = 2.0 * rate
        series = x * (1.0 - x * (1 / 2) * (1.0 - x * (1 / 3) * (1.0 - x * (1 / 4) * (1.0 - x * (1 / 5)))))
        amplitude = residue_ref[:, lanes] * jnp.sqrt(jnp.where(x < 0.05, series, 1.0 - jnp.exp(-x)))
        amplitude_ref[:, lanes] = amplitude
        rate = rate[:, None, :]
        step = jnp.broadcast_to(jnp.exp(-8.0 * rate), (MODES, 8, LANES))
        part = amplitude[:, None, :] * jnp.exp(-sub * rate)
        for j in range(BLOCK // 8):
            filt[8 * j : 8 * j + 8, own] = jnp.sum(part, axis=0)
            part = part * step
        filt[0:1, own] = filt[0:1, own] + skip_ref[0:1, lanes]
    taps = filt[...]
    high = taps.astype(BF16)
    low = (taps - high.astype(F32)).astype(BF16)
    lanes = lane_window(i, WIDE)
    long_spec[:, lanes] = dot(fwd_ref[:, :BLOCK], high) + dot(low_ref[...], high) + dot(fwd_ref[:, :BLOCK], low)


def block_states(second, rate_ref, local, blocks, i):
    sub = lax.broadcasted_iota(jnp.int32, (1, 8, 1), 1).astype(F32)
    for tile in range(WIDE // LANES):
        lanes = pl.ds(pl.multiple_of(i * WIDE + tile * LANES, LANES), LANES)
        rate = rate_ref[:, lanes][:, None, :]
        step = jnp.broadcast_to(jnp.exp(-8.0 * rate), (MODES, 8, LANES))
        weight = jnp.exp((sub - 8.0) * rate)
        for b in blocks:
            signal = second[b * BLOCK : (b + 1) * BLOCK, lanes].astype(F32)
            acc = jnp.broadcast_to(signal[0:8][None], (MODES, 8, LANES))
            for j in range(1, BLOCK // 8):
                acc = acc * step + signal[8 * j : 8 * j + 8][None]
            local[b, :, lanes] = sublane_sums(acc * weight)


def kernel_states(
    genome_ref, values_hbm, gate_one_hbm, gate_two_hbm, short_ref, taps_ref, rate_ref, residue_ref, skip_ref, fwd_ref, low_ref,
    back_ref, back_start_ref,
    intra_out, local_out, incoming_out, amplitude_out,
    values, gate_one, gate_two, first, second, halo, rim, taps_full, taps_spec, local, ends_own, ends, entering,
    fwd_keep, window, spec, product, amplitude, filt, long_spec, intra,
    load_sem, store_sem, rim_sem, halo_send, halo_recv, taps_send, taps_recv, ends_send, ends_recv, enter_send, enter_recv, intra_sem,
):
    rows, channels = values.shape
    count = rows // BLOCK
    chunks = channels // WIDE
    parts = lax.axis_size("seq")
    width = channels // parts
    per_chunk = WIDE // width
    dps = lax.axis_size("dp")
    chips = dps // 2
    seq = lax.axis_index("seq")
    dp = lax.axis_index("dp")
    chip, core = dp // 2, dp % 2
    twin = chip * 2 + (1 - core)
    following = lax.rem(seq + 1, parts)
    keeps = keep_scalars(genome_ref, seq, count)
    tail = rows - BLOCK

    def remote(src, dst, send, recv, dp_to, seq_to):
        return pltpu.make_async_remote_copy(
            src_ref=src, dst_ref=dst, send_sem=send, recv_sem=recv,
            device_id=(dp_to, seq_to), device_id_type=pl.DeviceIdType.MESH,
        )

    loads = []
    for src, dst, part in (
        (values_hbm, values, slice(tail - 16, rows)),
        (gate_one_hbm, gate_one, slice(tail, rows)),
        (values_hbm, values, slice(0, tail - 16)),
        (gate_one_hbm, gate_one, slice(0, tail)),
        (gate_two_hbm, gate_two, slice(0, rows)),
    ):
        copy = pltpu.make_async_copy(src.at[part], dst.at[part], load_sem.at[len(loads)])
        copy.start()
        loads.append(copy)

    barrier = pltpu.get_barrier_semaphore()
    peers = 0
    for k in range(1, parts):
        pl.semaphore_signal(
            barrier, inc=1, device_id=(dp, lax.rem(seq + k, parts)), device_id_type=pl.DeviceIdType.MESH
        )
        peers += 1
    for k in range(1, chips):
        pl.semaphore_signal(
            barrier, inc=1, device_id=(lax.rem(chip + k, chips) * 2 + core, seq), device_id_type=pl.DeviceIdType.MESH
        )
        peers += 1
    pl.semaphore_signal(barrier, inc=1, device_id=(twin, seq), device_id_type=pl.DeviceIdType.MESH)
    pl.semaphore_wait(barrier, peers + 1)

    rim_copy = remote(values_hbm.at[slice(rows - 16, rows)], rim, rim_sem.at[0], rim_sem.at[1], dp, following)
    rim_copy.start()

    def taps_copy(slot, index, src, dp_to):
        return remote(src, taps_full.at[slot], taps_send.at[index], taps_recv.at[slot], dp_to, seq)

    taps_own = pltpu.make_async_copy(taps_ref, taps_full.at[dp], taps_recv.at[dp])
    taps_own.start()
    taps_copies = [taps_copy(dp, k - 1, taps_ref, lax.rem(chip + k, chips) * 2 + core) for k in range(1, chips)]
    taps_copies.append(taps_copy(dp, chips - 1, taps_ref, twin))
    for copy in taps_copies:
        copy.start()

    loads[0].wait()
    loads[1].wait()

    def halo_copy(i):
        lanes = lane_window(i, WIDE)
        return remote(
            first.at[slice(tail, rows), lanes], halo.at[:, lanes], halo_send.at[i], halo_recv.at[i], dp, following
        )

    def tail_step(i, carry):
        short_block(
            values, lambda lanes: values[tail - 16 : tail, lanes], gate_one, short_ref, keeps[count - 1], window, first,
            slice(tail, rows), i,
        )
        halo_copy(i).start()
        return carry

    lax.fori_loop(0, chunks, tail_step, 0)

    for b in range(count):
        column = lax.broadcasted_iota(jnp.int32, fwd_ref.shape, 1)
        matrix = fwd_ref[...].astype(F32)
        fwd_keep[b] = jnp.where(column < BLOCK, matrix * keeps[b], matrix).astype(BF16)

    loads[2].wait()
    loads[3].wait()
    rim_copy.wait()

    def first_step(i, carry):
        for b in range(count - 1):
            start = b * BLOCK
            if b == 0:
                before = lambda lanes: rim[:, lanes]
            else:
                before = lambda lanes, start=start: values[start - 16 : start, lanes]
            short_block(values, before, gate_one, short_ref, keeps[b], window, first, slice(start, start + BLOCK), i)
        return carry

    lax.fori_loop(0, chunks, first_step, 0)

    def filter_step(i, carry):
        long_filter(rate_ref, residue_ref, skip_ref, fwd_ref, low_ref, amplitude, filt, long_spec, i)
        return carry

    lax.fori_loop(0, chunks, filter_step, 0)
    store_amplitude = pltpu.make_async_copy(amplitude, amplitude_out, store_sem.at[0])
    store_amplitude.start()

    forwards = []
    for k in range(1, chips):
        source = lax.rem(chip + k, chips) * 2 + core
        taps_copy(source, k - 1, taps_ref, source).wait_recv()
        copy = taps_copy(source, chips - 1 + k, taps_full.at[source], twin)
        copy.start()
        forwards.append(copy)
    taps_own.wait()
    for k in range(chips):
        source = lax.rem(chip + k, chips) * 2 + (1 - core)
        taps_copy(source, chips - 1, taps_ref, twin).wait_recv()
    loads[4].wait()

    def second_step(i, carry):
        lanes = lane_window(i, WIDE)
        taps = taps_full[i]
        taps_spec[:, lanes] = dot(fwd_ref[:, :BLOCK], taps) + dot(low_ref[...], taps)
        blocks = range(1, count)
        for b, medium in staged(
            lambda b: fwd_keep[b], lambda b: first[(b - 1) * BLOCK : (b + 1) * BLOCK, lanes], back_ref[...],
            lambda part: taps_spec[part, lanes], spec, product, blocks,
        ):
            part = slice(b * BLOCK, (b + 1) * BLOCK)
            second[part, lanes] = (gate_two[part, lanes].astype(F32) * medium).astype(BF16)
        block_states(second, rate_ref, local, blocks, i)
        return carry

    lax.fori_loop(0, chunks, second_step, 0)
    def ends_copy(part):
        return remote(ends_own.at[part], ends.at[seq], ends_send.at[part], ends_recv.at[seq], dp, part)

    def opening_step(pair, carry):
        both = [pair * 2, pair * 2 + 1]
        for h, i in enumerate(both):
            halo_copy(i).wait_recv()
        for h, i in enumerate(both):
            lanes = lane_window(i, WIDE)
            spec[h] = dot(fwd_keep[0, :, :BLOCK], halo[:, lanes]) + dot(fwd_keep[0, :, BLOCK:], first[0:BLOCK, lanes])
        for h, i in enumerate(both):
            lanes = lane_window(i, WIDE)
            pointwise(spec, product, lambda part: taps_spec[part, lanes], h)
        for h, i in enumerate(both):
            lanes = lane_window(i, WIDE)
            medium = dot(back_ref[...], product[h])
            second[0:BLOCK, lanes] = (gate_two[0:BLOCK, lanes].astype(F32) * medium).astype(BF16)
        for i in both:
            lanes = lane_window(i, WIDE)
            block_states(second, rate_ref, local, range(1), i)
            decay = jnp.exp(-float(BLOCK) * rate_ref[:, lanes])
            total = local[0, :, lanes]
            for b in range(1, count):
                total = keeps[b] * decay * total + local[b, :, lanes]
            for h in range(per_chunk):
                part = i * per_chunk + h
                ends_own[part] = total[:, h * width : (h + 1) * width]

                @pl.when(part != seq)
                def _():
                    ends_copy(part).start()

                @pl.when(part == seq)
                def _():
                    ends[part] = total[:, h * width : (h + 1) * width]

        return carry

    lax.fori_loop(0, chunks // 2, opening_step, 0)
    store_local = pltpu.make_async_copy(local, local_out, store_sem.at[1])
    store_local.start()

    def intra_copy(i):
        lanes = lane_window(i, WIDE)
        return pltpu.make_async_copy(intra.at[:, lanes], intra_out.at[:, lanes], intra_sem.at[i])

    def intra_step(i, carry):
        lanes = lane_window(i, WIDE)
        for b, result in staged(
            lambda b: fwd_ref[:, :BLOCK], lambda b: second[b * BLOCK : (b + 1) * BLOCK, lanes], back_start_ref[...],
            lambda part: long_spec[part, lanes], spec, product, range(count),
        ):
            intra[b * BLOCK : (b + 1) * BLOCK, lanes] = result
        intra_copy(i).start()
        return carry

    lax.fori_loop(0, chunks // 2, intra_step, 0)

    def arrival(k, carry):
        source = lax.rem(seq + k, parts)
        remote(ends_own.at[source], ends.at[source], ends_send.at[source], ends_recv.at[source], dp, source).wait_recv()
        return carry

    lax.fori_loop(1, parts, arrival, 0)

    begins = [jnp.int32(0)]
    for g in range(genome_ref.shape[1] - 1):
        begins.append(begins[-1] + genome_ref[0, g])
    decay = jnp.exp(-float(rows) * rate_ref[:, lane_window(seq, width)])

    def enter_copy(p):
        return remote(entering.at[p], incoming_out.at[seq], enter_send.at[p], enter_recv.at[seq], dp, p)

    def scan_step(p, state):
        entering[p] = state

        @pl.when(p != seq)
        def _():
            enter_copy(p).start()

        through = jnp.float32(1.0)
        for b in range(count):
            for begin in begins:
                through = jnp.where(p * count + b == begin, 0.0, through)
        return through * decay * state + ends[p]

    lax.fori_loop(0, parts, scan_step, jnp.zeros((MODES, width), F32))
    lax.fori_loop(chunks // 2, chunks, intra_step, 0)
    enter_own = pltpu.make_async_copy(entering.at[seq], incoming_out.at[seq], store_sem.at[2])
    enter_own.start()

    def departures(k, carry):
        other = lax.rem(seq + k, parts)
        ends_copy(other).wait_send()
        enter_copy(other).wait_send()
        remote(entering.at[other], incoming_out.at[other], enter_send.at[other], enter_recv.at[other], dp, other).wait_recv()
        return carry

    lax.fori_loop(1, parts, departures, 0)

    def halo_sent(i, carry):
        halo_copy(i).wait_send()
        intra_copy(i).wait()
        return carry

    lax.fori_loop(0, chunks, halo_sent, 0)
    for copy in taps_copies + forwards:
        copy.wait_send()
    for copy in (store_amplitude, store_local, enter_own):
        copy.wait()


def kernel_mixed(genome_ref, intra_ref, gate_ref, local_ref, incoming_ref, rate_ref, amplitude_ref, mixed_ref):
    count = intra_ref.shape[0] // BLOCK
    keeps = keep_scalars(genome_ref, lax.axis_index("seq"), count)
    sub = lax.broadcasted_iota(jnp.int32, (1, 8, 1), 1).astype(F32)
    width = incoming_ref.shape[2]
    for tile in range(WIDE // LANES):
        lanes = slice(tile * LANES, (tile + 1) * LANES)
        rate = rate_ref[:, lanes]
        decay = jnp.exp(-float(BLOCK) * rate)
        rate = rate[:, None, :]
        step = jnp.broadcast_to(jnp.exp(-8.0 * rate), (MODES, 8, LANES))
        weight = amplitude_ref[:, lanes][:, None, :] * jnp.exp(-sub * rate)
        piece, offset = tile * LANES // width, tile * LANES % width
        state = incoming_ref[piece, :, offset : offset + LANES]
        for b in range(count):
            state = state * keeps[b]
            part = weight * state[:, None, :]
            for j in range(0, BLOCK, 16):
                rows = slice(b * BLOCK + j, b * BLOCK + j + 16)
                upper = jnp.sum(part, axis=0)
                part = part * step
                lower = jnp.sum(part, axis=0)
                part = part * step
                total = intra_ref[rows, lanes].astype(F32) + jnp.concatenate([upper, lower], axis=0)
                mixed_ref[rows, lanes] = (gate_ref[rows, lanes].astype(F32) * total).astype(BF16)
            if b < count - 1:
                state = decay * state + local_ref[b, :, lanes]


def chunked(rows):
    return pl.BlockSpec((rows, WIDE), lambda i: (0, i))


def whole(shape):
    return pl.BlockSpec(shape, lambda i: (0,) * len(shape))


def body(values, gate_one, gate_two, gate_three, genome_blocks, short_taps, medium_taps, decay_rate, residue, long_skip):
    rows, channels = values.shape[1:]
    count = rows // BLOCK
    parts = lax.axis_size("seq")
    dps = lax.axis_size("dp")
    width = channels // parts
    chunks = channels // WIDE
    fwd, low, back_end, back_start = [jnp.asarray(m) for m in transform_matrices()]
    rate = decay_rate.T
    smem = pl.BlockSpec(memory_space=pltpu.SMEM)
    vmem = pl.BlockSpec(memory_space=pltpu.VMEM)
    hbm = pl.BlockSpec(memory_space=pl.ANY)
    stream = pltpu.VMEM((rows, channels), BF16)
    dma = pltpu.SemaphoreType.DMA

    intra, local, incoming, amplitude = pl.pallas_call(
        kernel_states,
        in_specs=[smem, hbm, hbm, hbm] + [vmem] * 9,
        out_specs=[hbm] * 4,
        out_shape=[
            jax.ShapeDtypeStruct((rows, channels), INTRA),
            jax.ShapeDtypeStruct((count, MODES, channels), F32),
            jax.ShapeDtypeStruct((parts, MODES, width), F32),
            jax.ShapeDtypeStruct((MODES, channels), F32),
        ],
        scratch_shapes=[
            stream, stream, stream, stream, stream,
            pltpu.VMEM((BLOCK, channels), BF16),
            pltpu.VMEM((16, channels), BF16),
            pltpu.VMEM((dps, BLOCK, WIDE), BF16),
            pltpu.VMEM((2 * BLOCK, channels), F32),
            pltpu.VMEM((count, MODES, channels), F32),
            pltpu.VMEM((parts, MODES, width), F32),
            pltpu.VMEM((parts, MODES, width), F32),
            pltpu.VMEM((parts, MODES, width), F32),
            pltpu.VMEM((count, 2 * BLOCK, 2 * BLOCK), BF16),
            pltpu.VMEM((WIDE // LANES, 16 + BLOCK, LANES), F32),
            pltpu.VMEM((count, 2 * BLOCK, WIDE), F32),
            pltpu.VMEM((count, 2 * BLOCK, WIDE), BF16),
            pltpu.VMEM((MODES, channels), F32),
            pltpu.VMEM((BLOCK, WIDE), F32),
            pltpu.VMEM((2 * BLOCK, channels), F32),
            pltpu.VMEM((rows, channels), INTRA),
            dma((5,)), dma((3,)), dma((2,)), dma((chunks,)), dma((chunks,)), dma((dps,)), dma((dps,)),
            dma((parts,)), dma((parts,)), dma((parts,)), dma((parts,)), dma((chunks,)),
        ],
        compiler_params=pltpu.CompilerParams(
            vmem_limit_bytes=VMEM_LIMIT, collective_id=0, has_side_effects=True
        ),
        name="states",
    )(
        genome_blocks, values[0], gate_one[0], gate_two[0], short_taps, medium_taps, rate, residue.T, long_skip[None],
        fwd, low, back_end, back_start,
    )

    per_chunk = WIDE // width
    mixed = pl.pallas_call(
        kernel_mixed,
        grid=(chunks,),
        in_specs=[
            smem, chunked(rows), chunked(rows), pl.BlockSpec((count, MODES, WIDE), lambda i: (0, 0, i)),
            pl.BlockSpec((per_chunk, MODES, width), lambda i: (i, 0, 0)),
            chunked(MODES), chunked(MODES),
        ],
        out_specs=chunked(rows),
        out_shape=jax.ShapeDtypeStruct((rows, channels), BF16),
        compiler_params=pltpu.CompilerParams(vmem_limit_bytes=VMEM_LIMIT),
        name="mixed",
    )(genome_blocks, intra, gate_three[0], local, incoming, rate, amplitude)
    return mixed[None]


def solution(mesh):
    return jax.shard_map(
        body,
        mesh=mesh,
        in_specs=(
            P("dp", "seq", None),
            P("dp", "seq", None),
            P("dp", "seq", None),
            P("dp", "seq", None),
            P("dp", None),
            P(),
            P(None, "dp"),
            P(),
            P(),
            P(),
        ),
        out_specs=P("dp", "seq", None),
        check_vma=False,
    )
```

```python
import functools

import jax
import jax.numpy as jnp
import numpy as np
from jax import lax
from jax.experimental import pallas as pl
from jax.experimental.pallas import tpu as pltpu
from jax.sharding import PartitionSpec as P

SHORT_TAPS = 7
MED_TAPS = 128
BLOCK = 128
WIDE = 512
MODES = 16
LANES = 128
F32 = jnp.float32
BF16 = jnp.bfloat16
INTRA = F32
VMEM_LIMIT = 58 * 1024 * 1024


def transform_matrices():
    n = np.arange(2 * BLOCK)
    j = np.arange(BLOCK)
    angle = np.pi * (2 * j + 1)[:, None] * n[None] / (2 * BLOCK)
    forward = np.concatenate([np.cos(angle), -np.sin(angle)], axis=0)
    backward = np.concatenate([np.cos(angle).T, -np.sin(angle).T], axis=1) / BLOCK
    high = forward.astype(jnp.bfloat16)
    low = (forward - high.astype(np.float64)).astype(jnp.bfloat16)
    return high, np.concatenate([high[:, :BLOCK], low[:, :BLOCK]], axis=1), backward[BLOCK:].astype(jnp.bfloat16), backward[:BLOCK].astype(jnp.bfloat16)


def keep_scalars(genome_ref, position, count):
    begins = [jnp.int32(0)]
    for g in range(genome_ref.shape[1] - 1):
        begins.append(begins[-1] + genome_ref[0, g])
    keeps = []
    for b in range(count):
        block = position * count + b
        starts = functools.reduce(jnp.logical_or, [block == begin for begin in begins])
        keeps.append(jnp.where(starts, 0.0, 1.0).astype(F32))
    return keeps


def dot(a, b):
    return jnp.dot(a, b, preferred_element_type=F32)


def pointwise(spec, product, taps_spec, b):
    for r in range(0, BLOCK, 16):
        re, im = slice(r, r + 16), slice(BLOCK + r, BLOCK + r + 16)
        wr, wi, tr, ti = spec[b, re], spec[b, im], taps_spec(re), taps_spec(im)
        product[b, re] = (wr * tr - wi * ti).astype(BF16)
        product[b, im] = (wr * ti + wi * tr).astype(BF16)


def staged(fwd_of, signal_of, back, taps_spec, spec, product, blocks):
    for b in blocks:
        spec[b] = dot(fwd_of(b), signal_of(b))
    for b in blocks:
        pointwise(spec, product, taps_spec, b)
    return [(b, dot(back, product[b])) for b in blocks]


def lane_window(i, width):
    return pl.ds(pl.multiple_of(i * width, width), width)


def short_block(values, before, gate, taps, keep, window, slot, first, rows, i):
    for tile in range(WIDE // LANES):
        lanes = pl.ds(pl.multiple_of(i * WIDE + tile * LANES, LANES), LANES)
        window[slot + tile, 0:16] = before(lanes).astype(F32) * keep
        window[slot + tile, 16 : 16 + BLOCK] = values[rows, lanes].astype(F32)
        weights = taps[:, lanes].astype(F32)
        total = window[slot + tile, 16 : 16 + BLOCK] * weights[0:1]
        for k in range(1, SHORT_TAPS):
            total = total + window[slot + tile, 16 - k : 16 - k + BLOCK] * weights[k : k + 1]
        first[rows, lanes] = (gate[rows, lanes].astype(F32) * total).astype(BF16)


def sublane_sums(stack):
    sub = lax.broadcasted_iota(jnp.int32, (8, LANES), 0)
    groups = []
    for g in range(0, MODES, 8):
        level = [stack[g + m] for m in range(8)]
        for shift in (1, 2, 4):
            low = (sub & shift) == 0
            level = [
                jnp.where(low, a, b) + pltpu.roll(jnp.where(low, b, a), shift, 0)
                for a, b in zip(level[0::2], level[1::2])
            ]
        groups.append(level[0])
    return jnp.concatenate(groups, axis=0)


def long_filter(rate_ref, residue_ref, skip_ref, fwd_ref, pair_ref, amplitude_ref, filt, long_spec, i):
    sub = lax.broadcasted_iota(jnp.int32, (1, 8, 1), 1).astype(F32)
    for tile in range(WIDE // LANES):
        own = slice(tile * LANES, (tile + 1) * LANES)
        lanes = pl.ds(pl.multiple_of(i * WIDE + tile * LANES, LANES), LANES)
        rate = rate_ref[:, lanes]
        x = 2.0 * rate
        series = x * (1.0 - x * (1 / 2) * (1.0 - x * (1 / 3) * (1.0 - x * (1 / 4) * (1.0 - x * (1 / 5)))))
        amplitude = residue_ref[:, lanes] * jnp.sqrt(jnp.where(x < 0.05, series, 1.0 - jnp.exp(-x)))
        amplitude_ref[:, lanes] = amplitude
        rate = rate[:, None, :]
        step = jnp.broadcast_to(jnp.exp(-8.0 * rate), (MODES, 8, LANES))
        part = amplitude[:, None, :] * jnp.exp(-sub * rate)
        for j in range(BLOCK // 8):
            filt[8 * j : 8 * j + 8, own] = jnp.sum(part, axis=0)
            part = part * step
        filt[0:1, own] = filt[0:1, own] + skip_ref[0:1, lanes]
    taps = filt[...]
    high = taps.astype(BF16)
    low = (taps - high.astype(F32)).astype(BF16)
    lanes = lane_window(i, WIDE)
    long_spec[:, lanes] = dot(pair_ref[...], jnp.concatenate([high, high], axis=0)) + dot(fwd_ref[:, :BLOCK], low)


def block_states(second, rate_ref, local, blocks, i):
    sub = lax.broadcasted_iota(jnp.int32, (1, 8, 1), 1).astype(F32)
    for tile in range(WIDE // LANES):
        lanes = pl.ds(pl.multiple_of(i * WIDE + tile * LANES, LANES), LANES)
        rate = rate_ref[:, lanes][:, None, :]
        step = jnp.broadcast_to(jnp.exp(-8.0 * rate), (MODES, 8, LANES))
        weight = jnp.exp((sub - 8.0) * rate)
        for b in blocks:
            signal = second[b * BLOCK : (b + 1) * BLOCK, lanes].astype(F32)
            acc = jnp.broadcast_to(signal[0:8][None], (MODES, 8, LANES))
            for j in range(1, BLOCK // 8):
                acc = acc * step + signal[8 * j : 8 * j + 8][None]
            local[b, :, lanes] = sublane_sums(acc * weight)


def kernel_states(
    genome_ref, values_hbm, gate_one_hbm, gate_two_hbm, short_hbm, taps_ref, rate_hbm, residue_hbm, skip_hbm, fwd_hbm, pair_hbm,
    back_hbm, back_start_hbm,
    intra_out, local_out, incoming_out, amplitude_out,
    values, gate_one, gate_two, first, second, halo, rim, taps_full, taps_spec, local, ends_own, ends, entering,
    fwd_keep, window, spec, product, amplitude, filt, long_spec, intra,
    short_ref, rate_ref, residue_ref, skip_ref, fwd_ref, pair_ref, back_ref, back_start_ref,
    small_sem, load_sem, store_sem, rim_sem, halo_send, halo_recv, taps_send, taps_recv, ends_send, ends_recv, enter_send, enter_recv, intra_sem,
):
    rows, channels = values.shape
    count = rows // BLOCK
    chunks = channels // WIDE
    parts = lax.axis_size("seq")
    width = channels // parts
    per_chunk = WIDE // width
    dps = lax.axis_size("dp")
    chips = dps // 2
    seq = lax.axis_index("seq")
    dp = lax.axis_index("dp")
    chip, core = dp // 2, dp % 2
    twin = chip * 2 + (1 - core)
    following = lax.rem(seq + 1, parts)
    keeps = keep_scalars(genome_ref, seq, count)
    tail = rows - BLOCK

    def remote(src, dst, send, recv, dp_to, seq_to):
        return pltpu.make_async_remote_copy(
            src_ref=src, dst_ref=dst, send_sem=send, recv_sem=recv,
            device_id=(dp_to, seq_to), device_id_type=pl.DeviceIdType.MESH,
        )

    loads = []
    for src, dst, part in (
        (values_hbm, values, slice(tail - 16, rows)),
        (gate_one_hbm, gate_one, slice(tail, rows)),
        (values_hbm, values, slice(0, tail - 16)),
        (gate_one_hbm, gate_one, slice(0, tail)),
        (gate_two_hbm, gate_two, slice(0, rows)),
    ):
        loads.append(pltpu.make_async_copy(src.at[part], dst.at[part], load_sem.at[len(loads)]))
    small = [
        pltpu.make_async_copy(src, dst, small_sem.at[n])
        for n, (src, dst) in enumerate(
            (
                (short_hbm, short_ref), (fwd_hbm, fwd_ref), (rate_hbm, rate_ref), (residue_hbm, residue_ref),
                (skip_hbm, skip_ref), (pair_hbm, pair_ref), (back_hbm, back_ref), (back_start_hbm, back_start_ref),
            )
        )
    ]
    small[0].start()
    loads[0].start()
    loads[1].start()
    for copy in small[1:]:
        copy.start()

    barrier = pltpu.get_barrier_semaphore()
    peers = 0
    for k in range(1, parts):
        pl.semaphore_signal(
            barrier, inc=1, device_id=(dp, lax.rem(seq + k, parts)), device_id_type=pl.DeviceIdType.MESH
        )
        peers += 1
    for k in range(1, chips):
        pl.semaphore_signal(
            barrier, inc=1, device_id=(lax.rem(chip + k, chips) * 2 + core, seq), device_id_type=pl.DeviceIdType.MESH
        )
        peers += 1
    pl.semaphore_signal(barrier, inc=1, device_id=(twin, seq), device_id_type=pl.DeviceIdType.MESH)
    pl.semaphore_wait(barrier, peers + 1)

    rim_copy = remote(values_hbm.at[slice(rows - 16, rows)], rim, rim_sem.at[0], rim_sem.at[1], dp, following)
    rim_copy.start()

    def taps_copy(slot, index, src, dp_to):
        return remote(src, taps_full.at[slot], taps_send.at[index], taps_recv.at[slot], dp_to, seq)

    taps_own = pltpu.make_async_copy(taps_ref, taps_full.at[dp], taps_recv.at[dp])
    taps_own.start()
    taps_copies = [taps_copy(dp, k - 1, taps_ref, lax.rem(chip + k, chips) * 2 + core) for k in range(1, chips)]
    taps_copies.append(taps_copy(dp, chips - 1, taps_ref, twin))
    for copy in taps_copies:
        copy.start()

    loads[0].wait()
    loads[1].wait()
    small[0].wait()
    for copy in loads[2:]:
        copy.start()

    def halo_copy(i):
        lanes = lane_window(i, WIDE)
        return remote(
            first.at[slice(tail, rows), lanes], halo.at[:, lanes], halo_send.at[i], halo_recv.at[i], dp, following
        )

    def tail_step(i, carry):
        short_block(
            values, lambda lanes: values[tail - 16 : tail, lanes], gate_one, short_ref, keeps[count - 1], window, 0, first,
            slice(tail, rows), i,
        )
        halo_copy(i).start()
        return carry

    lax.fori_loop(0, chunks, tail_step, 0)

    for copy in small[1:]:
        copy.wait()
    for b in range(count):
        column = lax.broadcasted_iota(jnp.int32, fwd_ref.shape, 1)
        matrix = fwd_ref[...].astype(F32)
        fwd_keep[b] = jnp.where(column < BLOCK, matrix * keeps[b], matrix).astype(BF16)

    def filter_step(i, carry):
        long_filter(rate_ref, residue_ref, skip_ref, fwd_ref, pair_ref, amplitude, filt, long_spec, i)
        return carry

    lax.fori_loop(0, chunks // 2, filter_step, 0)

    loads[2].wait()
    loads[3].wait()
    rim_copy.wait()

    def first_step(i, carry):
        for b in range(count - 1):
            start = b * BLOCK
            if b == 0:
                before = lambda lanes: rim[:, lanes]
            else:
                before = lambda lanes, start=start: values[start - 16 : start, lanes]
            short_block(
                values, before, gate_one, short_ref, keeps[b], window, b * (WIDE // LANES), first, slice(start, start + BLOCK), i
            )
        return carry

    lax.fori_loop(0, chunks, first_step, 0)

    forwards = []
    for k in range(1, chips):
        source = lax.rem(chip + k, chips) * 2 + core
        taps_copy(source, k - 1, taps_ref, source).wait_recv()
        copy = taps_copy(source, chips - 1 + k, taps_full.at[source], twin)
        copy.start()
        forwards.append(copy)
    taps_own.wait()
    for k in range(chips):
        source = lax.rem(chip + k, chips) * 2 + (1 - core)
        taps_copy(source, chips - 1, taps_ref, twin).wait_recv()
    loads[4].wait()

    def second_step(i, carry):
        lanes = lane_window(i, WIDE)
        taps = taps_full[i]
        taps_spec[:, lanes] = dot(pair_ref[...], jnp.concatenate([taps, taps], axis=0))
        blocks = range(1, count)
        for b, medium in staged(
            lambda b: fwd_keep[b], lambda b: first[(b - 1) * BLOCK : (b + 1) * BLOCK, lanes], back_ref[...],
            lambda part: taps_spec[part, lanes], spec, product, blocks,
        ):
            part = slice(b * BLOCK, (b + 1) * BLOCK)
            second[part, lanes] = (gate_two[part, lanes].astype(F32) * medium).astype(BF16)
        block_states(second, rate_ref, local, blocks, i)
        return carry

    lax.fori_loop(0, chunks, second_step, 0)
    def ends_copy(part):
        return remote(ends_own.at[part], ends.at[seq], ends_send.at[part], ends_recv.at[seq], dp, part)

    def opening_step(pair, carry):
        both = [pair * 2, pair * 2 + 1]
        for h, i in enumerate(both):
            halo_copy(i).wait_recv()
        for h, i in enumerate(both):
            lanes = lane_window(i, WIDE)
            spec[h] = dot(fwd_keep[0, :, :BLOCK], halo[:, lanes]) + dot(fwd_keep[0, :, BLOCK:], first[0:BLOCK, lanes])
        for h, i in enumerate(both):
            lanes = lane_window(i, WIDE)
            pointwise(spec, product, lambda part: taps_spec[part, lanes], h)
        for h, i in enumerate(both):
            lanes = lane_window(i, WIDE)
            medium = dot(back_ref[...], product[h])
            second[0:BLOCK, lanes] = (gate_two[0:BLOCK, lanes].astype(F32) * medium).astype(BF16)
        for i in both:
            lanes = lane_window(i, WIDE)
            block_states(second, rate_ref, local, range(1), i)
            decay = jnp.exp(-float(BLOCK) * rate_ref[:, lanes])
            total = local[0, :, lanes]
            for b in range(1, count):
                total = keeps[b] * decay * total + local[b, :, lanes]
            for h in range(per_chunk):
                part = i * per_chunk + h
                ends_own[part] = total[:, h * width : (h + 1) * width]

                @pl.when(part != seq)
                def _():
                    ends_copy(part).start()

                @pl.when(part == seq)
                def _():
                    ends[part] = total[:, h * width : (h + 1) * width]

        return carry

    lax.fori_loop(0, chunks // 2, opening_step, 0)
    store_local = pltpu.make_async_copy(local, local_out, store_sem.at[1])
    store_local.start()

    def intra_copy(i):
        lanes = lane_window(i, WIDE)
        return pltpu.make_async_copy(intra.at[:, lanes], intra_out.at[:, lanes], intra_sem.at[i])

    def intra_step(i, carry):
        lanes = lane_window(i, WIDE)
        for b, result in staged(
            lambda b: fwd_ref[:, :BLOCK], lambda b: second[b * BLOCK : (b + 1) * BLOCK, lanes], back_start_ref[...],
            lambda part: long_spec[part, lanes], spec, product, range(count),
        ):
            intra[b * BLOCK : (b + 1) * BLOCK, lanes] = result
        intra_copy(i).start()
        return carry

    lax.fori_loop(0, chunks // 2, intra_step, 0)
    lax.fori_loop(chunks // 2, chunks * 3 // 4, filter_step, 0)

    def arrival(k, carry):
        source = lax.rem(seq + k, parts)
        remote(ends_own.at[source], ends.at[source], ends_send.at[source], ends_recv.at[source], dp, source).wait_recv()
        return carry

    lax.fori_loop(1, parts, arrival, 0)

    begins = [jnp.int32(0)]
    for g in range(genome_ref.shape[1] - 1):
        begins.append(begins[-1] + genome_ref[0, g])
    decay = jnp.exp(-float(rows) * rate_ref[:, lane_window(seq, width)])

    def enter_copy(p):
        return remote(entering.at[p], incoming_out.at[seq], enter_send.at[p], enter_recv.at[seq], dp, p)

    def scan_step(p, state):
        entering[p] = state

        @pl.when(p != seq)
        def _():
            enter_copy(p).start()

        through = jnp.float32(1.0)
        for b in range(count):
            for begin in begins:
                through = jnp.where(p * count + b == begin, 0.0, through)
        return through * decay * state + ends[p]

    lax.fori_loop(0, parts, scan_step, jnp.zeros((MODES, width), F32))
    lax.fori_loop(chunks * 3 // 4, chunks, filter_step, 0)
    store_amplitude = pltpu.make_async_copy(amplitude, amplitude_out, store_sem.at[0])
    store_amplitude.start()
    lax.fori_loop(chunks // 2, chunks, intra_step, 0)
    enter_own = pltpu.make_async_copy(entering.at[seq], incoming_out.at[seq], store_sem.at[2])
    enter_own.start()

    def departures(k, carry):
        other = lax.rem(seq + k, parts)
        ends_copy(other).wait_send()
        enter_copy(other).wait_send()
        remote(entering.at[other], incoming_out.at[other], enter_send.at[other], enter_recv.at[other], dp, other).wait_recv()
        return carry

    lax.fori_loop(1, parts, departures, 0)

    def halo_sent(i, carry):
        halo_copy(i).wait_send()
        intra_copy(i).wait()
        return carry

    lax.fori_loop(0, chunks, halo_sent, 0)
    for copy in taps_copies + forwards:
        copy.wait_send()
    for copy in (store_amplitude, store_local, enter_own):
        copy.wait()


def kernel_mixed(genome_ref, intra_ref, gate_ref, local_ref, incoming_ref, rate_ref, amplitude_ref, mixed_ref):
    count = intra_ref.shape[0] // BLOCK
    keeps = keep_scalars(genome_ref, lax.axis_index("seq"), count)
    sub = lax.broadcasted_iota(jnp.int32, (1, 8, 1), 1).astype(F32)
    width = incoming_ref.shape[2]
    for tile in range(WIDE // LANES):
        lanes = slice(tile * LANES, (tile + 1) * LANES)
        rate = rate_ref[:, lanes]
        decay = jnp.exp(-float(BLOCK) * rate)
        rate = rate[:, None, :]
        step = jnp.broadcast_to(jnp.exp(-8.0 * rate), (MODES, 8, LANES))
        weight = amplitude_ref[:, lanes][:, None, :] * jnp.exp(-sub * rate)
        piece, offset = tile * LANES // width, tile * LANES % width
        state = incoming_ref[piece, :, offset : offset + LANES]
        for b in range(count):
            state = state * keeps[b]
            part = weight * state[:, None, :]
            for j in range(0, BLOCK, 16):
                rows = slice(b * BLOCK + j, b * BLOCK + j + 16)
                upper = jnp.sum(part, axis=0)
                part = part * step
                lower = jnp.sum(part, axis=0)
                part = part * step
                total = intra_ref[rows, lanes].astype(F32) + jnp.concatenate([upper, lower], axis=0)
                mixed_ref[rows, lanes] = (gate_ref[rows, lanes].astype(F32) * total).astype(BF16)
            if b < count - 1:
                state = decay * state + local_ref[b, :, lanes]


def chunked(rows):
    return pl.BlockSpec((rows, WIDE), lambda i: (0, i))


def whole(shape):
    return pl.BlockSpec(shape, lambda i: (0,) * len(shape))


def body(values, gate_one, gate_two, gate_three, genome_blocks, short_taps, medium_taps, decay_rate, residue, long_skip):
    rows, channels = values.shape[1:]
    count = rows // BLOCK
    parts = lax.axis_size("seq")
    dps = lax.axis_size("dp")
    width = channels // parts
    chunks = channels // WIDE
    fwd, pair, back_end, back_start = [jnp.asarray(m) for m in transform_matrices()]
    rate = decay_rate.T
    smem = pl.BlockSpec(memory_space=pltpu.SMEM)
    hbm = pl.BlockSpec(memory_space=pl.ANY)
    stream = pltpu.VMEM((rows, channels), BF16)
    dma = pltpu.SemaphoreType.DMA

    intra, local, incoming, amplitude = pl.pallas_call(
        kernel_states,
        in_specs=[smem] + [hbm] * 12,
        out_specs=[hbm] * 4,
        out_shape=[
            jax.ShapeDtypeStruct((rows, channels), INTRA),
            jax.ShapeDtypeStruct((count, MODES, channels), F32),
            jax.ShapeDtypeStruct((parts, MODES, width), F32),
            jax.ShapeDtypeStruct((MODES, channels), F32),
        ],
        scratch_shapes=[
            stream, stream, stream, stream, stream,
            pltpu.VMEM((BLOCK, channels), BF16),
            pltpu.VMEM((16, channels), BF16),
            pltpu.VMEM((dps, BLOCK, WIDE), BF16),
            pltpu.VMEM((2 * BLOCK, channels), F32),
            pltpu.VMEM((count, MODES, channels), F32),
            pltpu.VMEM((parts, MODES, width), F32),
            pltpu.VMEM((parts, MODES, width), F32),
            pltpu.VMEM((parts, MODES, width), F32),
            pltpu.VMEM((count, 2 * BLOCK, 2 * BLOCK), BF16),
            pltpu.VMEM((count * (WIDE // LANES), 16 + BLOCK, LANES), F32),
            pltpu.VMEM((count, 2 * BLOCK, WIDE), F32),
            pltpu.VMEM((count, 2 * BLOCK, WIDE), BF16),
            pltpu.VMEM((MODES, channels), F32),
            pltpu.VMEM((BLOCK, WIDE), F32),
            pltpu.VMEM((2 * BLOCK, channels), F32),
            pltpu.VMEM((rows, channels), INTRA),
            pltpu.VMEM((SHORT_TAPS, channels), BF16),
            pltpu.VMEM((MODES, channels), F32),
            pltpu.VMEM((MODES, channels), F32),
            pltpu.VMEM((1, channels), F32),
            pltpu.VMEM(fwd.shape, BF16),
            pltpu.VMEM(pair.shape, BF16),
            pltpu.VMEM(back_end.shape, BF16),
            pltpu.VMEM(back_start.shape, BF16),
            dma((8,)), dma((5,)), dma((3,)), dma((2,)), dma((chunks,)), dma((chunks,)), dma((dps,)), dma((dps,)),
            dma((parts,)), dma((parts,)), dma((parts,)), dma((parts,)), dma((chunks,)),
        ],
        compiler_params=pltpu.CompilerParams(
            vmem_limit_bytes=VMEM_LIMIT, collective_id=0, has_side_effects=True
        ),
        name="states",
    )(
        genome_blocks, values[0], gate_one[0], gate_two[0], short_taps, medium_taps, rate, residue.T, long_skip[None],
        fwd, pair, back_end, back_start,
    )

    per_chunk = WIDE // width
    mixed = pl.pallas_call(
        kernel_mixed,
        grid=(chunks,),
        in_specs=[
            smem, chunked(rows), chunked(rows), pl.BlockSpec((count, MODES, WIDE), lambda i: (0, 0, i)),
            pl.BlockSpec((per_chunk, MODES, width), lambda i: (i, 0, 0)),
            chunked(MODES), chunked(MODES),
        ],
        out_specs=chunked(rows),
        out_shape=jax.ShapeDtypeStruct((rows, channels), BF16),
        compiler_params=pltpu.CompilerParams(vmem_limit_bytes=VMEM_LIMIT),
        name="mixed",
    )(genome_blocks, intra, gate_three[0], local, incoming, rate, amplitude)
    return mixed[None]


def solution(mesh):
    return jax.shard_map(
        body,
        mesh=mesh,
        in_specs=(
            P("dp", "seq", None),
            P("dp", "seq", None),
            P("dp", "seq", None),
            P("dp", "seq", None),
            P("dp", None),
            P(),
            P(None, "dp"),
            P(),
            P(),
            P(),
        ),
        out_specs=P("dp", "seq", None),
        check_vma=False,
    )
```

```python
import functools

import jax
import jax.numpy as jnp
import numpy as np
from jax import lax
from jax.experimental import pallas as pl
from jax.experimental.pallas import tpu as pltpu
from jax.sharding import PartitionSpec as P

SHORT_TAPS = 7
MED_TAPS = 128
BLOCK = 128
WIDE = 512
MODES = 16
LANES = 128
F32 = jnp.float32
BF16 = jnp.bfloat16
INTRA = BF16
VMEM_LIMIT = 58 * 1024 * 1024


def transform_matrices():
    n = np.arange(2 * BLOCK)
    j = np.arange(BLOCK)
    angle = np.pi * (2 * j + 1)[:, None] * n[None] / (2 * BLOCK)
    forward = np.concatenate([np.cos(angle), -np.sin(angle)], axis=0)
    backward = np.concatenate([np.cos(angle).T, -np.sin(angle).T], axis=1) / BLOCK
    high = forward.astype(jnp.bfloat16)
    low = (forward - high.astype(np.float64)).astype(jnp.bfloat16)
    return high, np.concatenate([high[:, :BLOCK], low[:, :BLOCK]], axis=1), backward[BLOCK:].astype(jnp.bfloat16), backward[:BLOCK].astype(jnp.bfloat16)


def keep_scalars(genome_ref, position, count):
    begins = [jnp.int32(0)]
    for g in range(genome_ref.shape[1] - 1):
        begins.append(begins[-1] + genome_ref[0, g])
    keeps = []
    for b in range(count):
        block = position * count + b
        starts = functools.reduce(jnp.logical_or, [block == begin for begin in begins])
        keeps.append(jnp.where(starts, 0.0, 1.0).astype(F32))
    return keeps


def dot(a, b):
    return jnp.dot(a, b, preferred_element_type=F32)


def pointwise(spec, product, taps_spec, b):
    for r in range(0, BLOCK, 16):
        re, im = slice(r, r + 16), slice(BLOCK + r, BLOCK + r + 16)
        wr, wi, tr, ti = spec[b, re], spec[b, im], taps_spec(re), taps_spec(im)
        product[b, re] = (wr * tr - wi * ti).astype(BF16)
        product[b, im] = (wr * ti + wi * tr).astype(BF16)


def staged(fwd_of, signal_of, back, taps_spec, spec, product, blocks):
    for b in blocks:
        spec[b] = dot(fwd_of(b), signal_of(b))
    for b in blocks:
        pointwise(spec, product, taps_spec, b)
    for b in blocks:
        yield b, dot(back, product[b])


def lane_window(i, width):
    return pl.ds(pl.multiple_of(i * width, width), width)


def short_block(values, before, gate, taps, keep, window, slot, first, rows, i):
    for tile in range(WIDE // LANES):
        lanes = pl.ds(pl.multiple_of(i * WIDE + tile * LANES, LANES), LANES)
        window[slot + tile, 0:16] = before(lanes).astype(F32) * keep
        window[slot + tile, 16 : 16 + BLOCK] = values[rows, lanes].astype(F32)
        weights = taps[:, lanes].astype(F32)
        total = window[slot + tile, 16 : 16 + BLOCK] * weights[0:1]
        for k in range(1, SHORT_TAPS):
            total = total + window[slot + tile, 16 - k : 16 - k + BLOCK] * weights[k : k + 1]
        shifted = slice(rows.start + BLOCK, rows.stop + BLOCK)
        first[shifted, lanes] = (gate[rows, lanes].astype(F32) * total).astype(BF16)


def sublane_sums(stack):
    sub = lax.broadcasted_iota(jnp.int32, (8, LANES), 0)
    groups = []
    for g in range(0, MODES, 8):
        level = [stack[g + m] for m in range(8)]
        for shift in (1, 2, 4):
            low = (sub & shift) == 0
            level = [
                jnp.where(low, a, b) + pltpu.roll(jnp.where(low, b, a), shift, 0)
                for a, b in zip(level[0::2], level[1::2])
            ]
        groups.append(level[0])
    return jnp.concatenate(groups, axis=0)


def long_filter(rate_ref, residue_ref, skip_ref, fwd_ref, pair_ref, amplitude_ref, filt, long_spec, i):
    sub = lax.broadcasted_iota(jnp.int32, (1, 8, 1), 1).astype(F32)
    for tile in range(WIDE // LANES):
        own = slice(tile * LANES, (tile + 1) * LANES)
        lanes = pl.ds(pl.multiple_of(i * WIDE + tile * LANES, LANES), LANES)
        rate = rate_ref[:, lanes]
        x = 2.0 * rate
        series = x * (1.0 - x * (1 / 2) * (1.0 - x * (1 / 3) * (1.0 - x * (1 / 4) * (1.0 - x * (1 / 5)))))
        amplitude = residue_ref[:, lanes] * jnp.sqrt(jnp.where(x < 0.05, series, 1.0 - jnp.exp(-x)))
        amplitude_ref[:, lanes] = amplitude
        rate = rate[:, None, :]
        step = jnp.broadcast_to(jnp.exp(-8.0 * rate), (MODES, 8, LANES))
        part = amplitude[:, None, :] * jnp.exp(-sub * rate)
        for j in range(BLOCK // 8):
            filt[8 * j : 8 * j + 8, own] = jnp.sum(part, axis=0)
            part = part * step
        filt[0:1, own] = filt[0:1, own] + skip_ref[0:1, lanes]
    high = filt[...].astype(BF16)
    lanes = lane_window(i, WIDE)
    long_spec[:, lanes] = dot(pair_ref[...], jnp.concatenate([high, high], axis=0))


def block_states(second, rate_ref, local, blocks, i):
    sub = lax.broadcasted_iota(jnp.int32, (1, 8, 1), 1).astype(F32)
    for tile in range(WIDE // LANES):
        lanes = pl.ds(pl.multiple_of(i * WIDE + tile * LANES, LANES), LANES)
        rate = rate_ref[:, lanes][:, None, :]
        step = jnp.broadcast_to(jnp.exp(-8.0 * rate), (MODES, 8, LANES))
        weight = jnp.exp((sub - 8.0) * rate)
        for b in blocks:
            signal = second[b * BLOCK : (b + 1) * BLOCK, lanes].astype(F32)
            acc = jnp.broadcast_to(signal[0:8][None], (MODES, 8, LANES))
            for j in range(1, BLOCK // 8):
                acc = acc * step + signal[8 * j : 8 * j + 8][None]
            local[b, :, lanes] = sublane_sums(acc * weight)


def kernel_states(
    genome_ref, values_hbm, gate_one_hbm, gate_two_hbm, short_hbm, taps_ref, rate_hbm, residue_hbm, skip_hbm, fwd_hbm, pair_hbm,
    back_hbm, back_start_hbm,
    intra_out, local_out, incoming_out, amplitude_out,
    values, gate_one, gate_two, first, second, rim, taps_full, taps_spec, local, ends_own, ends, entering,
    fwd_keep, window, spec, product, amplitude, filt, long_spec, intra,
    short_ref, rate_ref, residue_ref, skip_ref, fwd_ref, pair_ref, back_ref, back_start_ref,
    small_sem, load_sem, store_sem, rim_sem, halo_send, halo_recv, taps_send, taps_recv, ends_send, ends_recv, enter_send, enter_recv, intra_sem,
):
    rows, channels = values.shape
    count = rows // BLOCK
    chunks = channels // WIDE
    parts = lax.axis_size("seq")
    width = channels // parts
    per_chunk = WIDE // width
    dps = lax.axis_size("dp")
    chips = dps // 2
    seq = lax.axis_index("seq")
    dp = lax.axis_index("dp")
    chip, core = dp // 2, dp % 2
    twin = chip * 2 + (1 - core)
    following = lax.rem(seq + 1, parts)
    keeps = keep_scalars(genome_ref, seq, count)
    tail = rows - BLOCK

    def remote(src, dst, send, recv, dp_to, seq_to):
        return pltpu.make_async_remote_copy(
            src_ref=src, dst_ref=dst, send_sem=send, recv_sem=recv,
            device_id=(dp_to, seq_to), device_id_type=pl.DeviceIdType.MESH,
        )

    loads = []
    for src, dst, part in (
        (values_hbm, values, slice(tail - 16, rows)),
        (gate_one_hbm, gate_one, slice(tail, rows)),
        (values_hbm, values, slice(0, tail - 16)),
        (gate_one_hbm, gate_one, slice(0, tail)),
        (gate_two_hbm, gate_two, slice(0, rows)),
    ):
        loads.append(pltpu.make_async_copy(src.at[part], dst.at[part], load_sem.at[len(loads)]))
    small = [
        pltpu.make_async_copy(src, dst, small_sem.at[n])
        for n, (src, dst) in enumerate(
            (
                (short_hbm, short_ref), (fwd_hbm, fwd_ref), (rate_hbm, rate_ref), (residue_hbm, residue_ref),
                (skip_hbm, skip_ref), (pair_hbm, pair_ref), (back_hbm, back_ref), (back_start_hbm, back_start_ref),
            )
        )
    ]
    small[0].start()
    loads[0].start()
    loads[1].start()
    for copy in small[1:]:
        copy.start()

    barrier = pltpu.get_barrier_semaphore()
    peers = 0
    for k in range(1, parts):
        pl.semaphore_signal(
            barrier, inc=1, device_id=(dp, lax.rem(seq + k, parts)), device_id_type=pl.DeviceIdType.MESH
        )
        peers += 1
    for k in range(1, chips):
        pl.semaphore_signal(
            barrier, inc=1, device_id=(lax.rem(chip + k, chips) * 2 + core, seq), device_id_type=pl.DeviceIdType.MESH
        )
        peers += 1
    pl.semaphore_signal(barrier, inc=1, device_id=(twin, seq), device_id_type=pl.DeviceIdType.MESH)
    pl.semaphore_wait(barrier, peers + 1)

    rim_copy = remote(values_hbm.at[slice(rows - 16, rows)], rim, rim_sem.at[0], rim_sem.at[1], dp, following)
    rim_copy.start()

    def taps_copy(slot, index, src, dp_to):
        return remote(src, taps_full.at[slot], taps_send.at[index], taps_recv.at[slot], dp_to, seq)

    taps_own = pltpu.make_async_copy(taps_ref, taps_full.at[dp], taps_recv.at[dp])
    taps_own.start()
    taps_copies = [taps_copy(dp, k - 1, taps_ref, lax.rem(chip + k, chips) * 2 + core) for k in range(1, chips)]
    taps_copies.append(taps_copy(dp, chips - 1, taps_ref, twin))
    for copy in taps_copies:
        copy.start()

    loads[0].wait()
    loads[1].wait()
    small[0].wait()
    for copy in loads[2:]:
        copy.start()

    def halo_copy(i):
        lanes = lane_window(i, WIDE)
        return remote(
            first.at[slice(rows, rows + BLOCK), lanes], first.at[slice(0, BLOCK), lanes], halo_send.at[i], halo_recv.at[i], dp, following
        )

    def tail_step(i, carry):
        short_block(
            values, lambda lanes: values[tail - 16 : tail, lanes], gate_one, short_ref, keeps[count - 1], window, 0, first,
            slice(tail, rows), i,
        )
        halo_copy(i).start()
        return carry

    lax.fori_loop(0, chunks, tail_step, 0)

    for copy in small[1:]:
        copy.wait()
    for b in range(count):
        column = lax.broadcasted_iota(jnp.int32, fwd_ref.shape, 1)
        matrix = fwd_ref[...].astype(F32)
        fwd_keep[b] = jnp.where(column < BLOCK, matrix * keeps[b], matrix).astype(BF16)

    def filter_step(i, carry):
        long_filter(rate_ref, residue_ref, skip_ref, fwd_ref, pair_ref, amplitude, filt, long_spec, i)
        return carry

    lax.fori_loop(0, chunks // 2, filter_step, 0)

    loads[2].wait()
    loads[3].wait()
    rim_copy.wait()

    def first_step(i, carry):
        for b in range(count - 1):
            start = b * BLOCK
            if b == 0:
                before = lambda lanes: rim[:, lanes]
            else:
                before = lambda lanes, start=start: values[start - 16 : start, lanes]
            short_block(
                values, before, gate_one, short_ref, keeps[b], window, b * (WIDE // LANES), first, slice(start, start + BLOCK), i
            )
        return carry

    lax.fori_loop(0, chunks, first_step, 0)

    forwards = []
    for k in range(1, chips):
        source = lax.rem(chip + k, chips) * 2 + core
        taps_copy(source, k - 1, taps_ref, source).wait_recv()
        copy = taps_copy(source, chips - 1 + k, taps_full.at[source], twin)
        copy.start()
        forwards.append(copy)
    taps_own.wait()
    for k in range(chips):
        source = lax.rem(chip + k, chips) * 2 + (1 - core)
        taps_copy(source, chips - 1, taps_ref, twin).wait_recv()
    loads[4].wait()

    def second_step(i, carry):
        lanes = lane_window(i, WIDE)
        taps = taps_full[i]
        taps_spec[:, lanes] = dot(pair_ref[...], jnp.concatenate([taps, taps], axis=0))
        blocks = range(1, count)
        for b, medium in staged(
            lambda b: fwd_keep[b], lambda b: first[b * BLOCK : (b + 2) * BLOCK, lanes], back_ref[...],
            lambda part: taps_spec[part, lanes], spec, product, blocks,
        ):
            part = slice(b * BLOCK, (b + 1) * BLOCK)
            second[part, lanes] = (gate_two[part, lanes].astype(F32) * medium).astype(BF16)
        block_states(second, rate_ref, local, blocks, i)
        return carry

    lax.fori_loop(0, chunks, second_step, 0)
    def ends_copy(part):
        return remote(ends_own.at[part], ends.at[seq], ends_send.at[part], ends_recv.at[seq], dp, part)

    def opening_step(pair, carry):
        both = [pair * 2, pair * 2 + 1]
        for h, i in enumerate(both):
            halo_copy(i).wait_recv()
        for h, i in enumerate(both):
            lanes = lane_window(i, WIDE)
            spec[h] = dot(fwd_keep[0], first[0 : 2 * BLOCK, lanes])
        for h, i in enumerate(both):
            lanes = lane_window(i, WIDE)
            pointwise(spec, product, lambda part: taps_spec[part, lanes], h)
        for h, i in enumerate(both):
            lanes = lane_window(i, WIDE)
            medium = dot(back_ref[...], product[h])
            second[0:BLOCK, lanes] = (gate_two[0:BLOCK, lanes].astype(F32) * medium).astype(BF16)
        for i in both:
            lanes = lane_window(i, WIDE)
            block_states(second, rate_ref, local, range(1), i)
            decay = jnp.exp(-float(BLOCK) * rate_ref[:, lanes])
            total = local[0, :, lanes]
            for b in range(1, count):
                total = keeps[b] * decay * total + local[b, :, lanes]
            for h in range(per_chunk):
                part = i * per_chunk + h
                ends_own[part] = total[:, h * width : (h + 1) * width]

                @pl.when(part != seq)
                def _():
                    ends_copy(part).start()

                @pl.when(part == seq)
                def _():
                    ends[part] = total[:, h * width : (h + 1) * width]

        return carry

    lax.fori_loop(0, chunks // 2, opening_step, 0)
    store_local = pltpu.make_async_copy(local, local_out, store_sem.at[1])
    store_local.start()

    def intra_copy(i):
        lanes = lane_window(i, WIDE)
        return pltpu.make_async_copy(intra.at[:, lanes], intra_out.at[:, lanes], intra_sem.at[i])

    def intra_step(i, carry):
        lanes = lane_window(i, WIDE)
        for b, result in staged(
            lambda b: fwd_ref[:, :BLOCK], lambda b: second[b * BLOCK : (b + 1) * BLOCK, lanes], back_start_ref[...],
            lambda part: long_spec[part, lanes], spec, product, range(count),
        ):
            intra[b * BLOCK : (b + 1) * BLOCK, lanes] = result.astype(INTRA)
        intra_copy(i).start()
        return carry

    lax.fori_loop(0, chunks // 2, intra_step, 0)
    lax.fori_loop(chunks // 2, chunks * 3 // 4, filter_step, 0)

    def arrival(k, carry):
        source = lax.rem(seq + k, parts)
        remote(ends_own.at[source], ends.at[source], ends_send.at[source], ends_recv.at[source], dp, source).wait_recv()
        return carry

    lax.fori_loop(1, parts, arrival, 0)

    begins = [jnp.int32(0)]
    for g in range(genome_ref.shape[1] - 1):
        begins.append(begins[-1] + genome_ref[0, g])
    decay = jnp.exp(-float(rows) * rate_ref[:, lane_window(seq, width)])

    def enter_copy(p):
        return remote(entering.at[p], incoming_out.at[seq], enter_send.at[p], enter_recv.at[seq], dp, p)

    def scan_step(p, state):
        entering[p] = state

        @pl.when(p != seq)
        def _():
            enter_copy(p).start()

        through = jnp.float32(1.0)
        for b in range(count):
            for begin in begins:
                through = jnp.where(p * count + b == begin, 0.0, through)
        return through * decay * state + ends[p]

    lax.fori_loop(0, parts, scan_step, jnp.zeros((MODES, width), F32))
    lax.fori_loop(chunks * 3 // 4, chunks, filter_step, 0)
    store_amplitude = pltpu.make_async_copy(amplitude, amplitude_out, store_sem.at[0])
    store_amplitude.start()
    lax.fori_loop(chunks // 2, chunks, intra_step, 0)
    enter_own = pltpu.make_async_copy(entering.at[seq], incoming_out.at[seq], store_sem.at[2])
    enter_own.start()

    def departures(k, carry):
        other = lax.rem(seq + k, parts)
        ends_copy(other).wait_send()
        enter_copy(other).wait_send()
        remote(entering.at[other], incoming_out.at[other], enter_send.at[other], enter_recv.at[other], dp, other).wait_recv()
        return carry

    lax.fori_loop(1, parts, departures, 0)

    def halo_sent(i, carry):
        halo_copy(i).wait_send()
        intra_copy(i).wait()
        return carry

    lax.fori_loop(0, chunks, halo_sent, 0)
    for copy in taps_copies + forwards:
        copy.wait_send()
    for copy in (store_amplitude, store_local, enter_own):
        copy.wait()


def kernel_mixed(genome_ref, intra_ref, gate_ref, local_ref, incoming_ref, rate_ref, amplitude_ref, mixed_ref):
    count = intra_ref.shape[0] // BLOCK
    keeps = keep_scalars(genome_ref, lax.axis_index("seq"), count)
    sub = lax.broadcasted_iota(jnp.int32, (1, 8, 1), 1).astype(F32)
    width = incoming_ref.shape[2]
    for tile in range(WIDE // LANES):
        lanes = slice(tile * LANES, (tile + 1) * LANES)
        rate = rate_ref[:, lanes]
        decay = jnp.exp(-float(BLOCK) * rate)
        rate = rate[:, None, :]
        step = jnp.broadcast_to(jnp.exp(-8.0 * rate), (MODES, 8, LANES))
        weight = amplitude_ref[:, lanes][:, None, :] * jnp.exp(-sub * rate)
        piece, offset = tile * LANES // width, tile * LANES % width
        state = incoming_ref[piece, :, offset : offset + LANES]
        for b in range(count):
            state = state * keeps[b]
            part = weight * state[:, None, :]
            for j in range(0, BLOCK, 16):
                rows = slice(b * BLOCK + j, b * BLOCK + j + 16)
                upper = jnp.sum(part, axis=0)
                part = part * step
                lower = jnp.sum(part, axis=0)
                part = part * step
                total = intra_ref[rows, lanes].astype(F32) + jnp.concatenate([upper, lower], axis=0)
                mixed_ref[rows, lanes] = (gate_ref[rows, lanes].astype(F32) * total).astype(BF16)
            if b < count - 1:
                state = decay * state + local_ref[b, :, lanes]


def chunked(rows):
    return pl.BlockSpec((rows, WIDE), lambda i: (0, i))


def whole(shape):
    return pl.BlockSpec(shape, lambda i: (0,) * len(shape))


def body(values, gate_one, gate_two, gate_three, genome_blocks, short_taps, medium_taps, decay_rate, residue, long_skip):
    rows, channels = values.shape[1:]
    count = rows // BLOCK
    parts = lax.axis_size("seq")
    dps = lax.axis_size("dp")
    width = channels // parts
    chunks = channels // WIDE
    fwd, pair, back_end, back_start = [jnp.asarray(m) for m in transform_matrices()]
    rate = decay_rate.T
    smem = pl.BlockSpec(memory_space=pltpu.SMEM)
    hbm = pl.BlockSpec(memory_space=pl.ANY)
    stream = pltpu.VMEM((rows, channels), BF16)
    dma = pltpu.SemaphoreType.DMA

    intra, local, incoming, amplitude = pl.pallas_call(
        kernel_states,
        in_specs=[smem] + [hbm] * 12,
        out_specs=[hbm] * 4,
        out_shape=[
            jax.ShapeDtypeStruct((rows, channels), INTRA),
            jax.ShapeDtypeStruct((count, MODES, channels), F32),
            jax.ShapeDtypeStruct((parts, MODES, width), F32),
            jax.ShapeDtypeStruct((MODES, channels), F32),
        ],
        scratch_shapes=[
            stream, stream, stream,
            pltpu.VMEM((rows + BLOCK, channels), BF16),
            stream,
            pltpu.VMEM((16, channels), BF16),
            pltpu.VMEM((dps, BLOCK, WIDE), BF16),
            pltpu.VMEM((2 * BLOCK, channels), F32),
            pltpu.VMEM((count, MODES, channels), F32),
            pltpu.VMEM((parts, MODES, width), F32),
            pltpu.VMEM((parts, MODES, width), F32),
            pltpu.VMEM((parts, MODES, width), F32),
            pltpu.VMEM((count, 2 * BLOCK, 2 * BLOCK), BF16),
            pltpu.VMEM((count * (WIDE // LANES), 16 + BLOCK, LANES), F32),
            pltpu.VMEM((count, 2 * BLOCK, WIDE), F32),
            pltpu.VMEM((count, 2 * BLOCK, WIDE), BF16),
            pltpu.VMEM((MODES, channels), F32),
            pltpu.VMEM((BLOCK, WIDE), F32),
            pltpu.VMEM((2 * BLOCK, channels), F32),
            pltpu.VMEM((rows, channels), INTRA),
            pltpu.VMEM((SHORT_TAPS, channels), BF16),
            pltpu.VMEM((MODES, channels), F32),
            pltpu.VMEM((MODES, channels), F32),
            pltpu.VMEM((1, channels), F32),
            pltpu.VMEM(fwd.shape, BF16),
            pltpu.VMEM(pair.shape, BF16),
            pltpu.VMEM(back_end.shape, BF16),
            pltpu.VMEM(back_start.shape, BF16),
            dma((8,)), dma((5,)), dma((3,)), dma((2,)), dma((chunks,)), dma((chunks,)), dma((dps,)), dma((dps,)),
            dma((parts,)), dma((parts,)), dma((parts,)), dma((parts,)), dma((chunks,)),
        ],
        compiler_params=pltpu.CompilerParams(
            vmem_limit_bytes=VMEM_LIMIT, collective_id=0, has_side_effects=True
        ),
        name="states",
    )(
        genome_blocks, values[0], gate_one[0], gate_two[0], short_taps, medium_taps, rate, residue.T, long_skip[None],
        fwd, pair, back_end, back_start,
    )

    per_chunk = WIDE // width
    mixed = pl.pallas_call(
        kernel_mixed,
        grid=(chunks,),
        in_specs=[
            smem, chunked(rows), chunked(rows), pl.BlockSpec((count, MODES, WIDE), lambda i: (0, 0, i)),
            pl.BlockSpec((per_chunk, MODES, width), lambda i: (i, 0, 0)),
            chunked(MODES), chunked(MODES),
        ],
        out_specs=chunked(rows),
        out_shape=jax.ShapeDtypeStruct((rows, channels), BF16),
        compiler_params=pltpu.CompilerParams(vmem_limit_bytes=VMEM_LIMIT),
        name="mixed",
    )(genome_blocks, intra, gate_three[0], local, incoming, rate, amplitude)
    return mixed[None]


def solution(mesh):
    return jax.shard_map(
        body,
        mesh=mesh,
        in_specs=(
            P("dp", "seq", None),
            P("dp", "seq", None),
            P("dp", "seq", None),
            P("dp", "seq", None),
            P("dp", None),
            P(),
            P(None, "dp"),
            P(),
            P(),
            P(),
        ),
        out_specs=P("dp", "seq", None),
        check_vma=False,
    )
```

```python
import functools

import jax
import jax.numpy as jnp
import numpy as np
from jax import lax
from jax.experimental import pallas as pl
from jax.experimental.pallas import tpu as pltpu
from jax.sharding import PartitionSpec as P

SHORT_TAPS = 7
MED_TAPS = 128
BLOCK = 128
WIDE = 512
MODES = 16
LANES = 128
F32 = jnp.float32
BF16 = jnp.bfloat16
INTRA = BF16
VMEM_LIMIT = 58 * 1024 * 1024


def transform_matrices():
    n = np.arange(2 * BLOCK)
    j = np.arange(BLOCK)
    angle = np.pi * (2 * j + 1)[:, None] * n[None] / (2 * BLOCK)
    forward = np.concatenate([np.cos(angle), -np.sin(angle)], axis=0)
    backward = np.concatenate([np.cos(angle).T, -np.sin(angle).T], axis=1) / BLOCK
    high = forward.astype(jnp.bfloat16)
    low = (forward - high.astype(np.float64)).astype(jnp.bfloat16)
    return high, np.concatenate([high[:, :BLOCK], low[:, :BLOCK]], axis=1), backward[BLOCK:].astype(jnp.bfloat16), backward[:BLOCK].astype(jnp.bfloat16)


def keep_scalars(genome_ref, position, count):
    begins = [jnp.int32(0)]
    for g in range(genome_ref.shape[1] - 1):
        begins.append(begins[-1] + genome_ref[0, g])
    keeps = []
    for b in range(count):
        block = position * count + b
        starts = functools.reduce(jnp.logical_or, [block == begin for begin in begins])
        keeps.append(jnp.where(starts, 0.0, 1.0).astype(F32))
    return keeps


def dot(a, b):
    return jnp.dot(a, b, preferred_element_type=F32)


def pointwise(spec, product, taps_spec, b):
    for r in range(0, BLOCK, 16):
        re, im = slice(r, r + 16), slice(BLOCK + r, BLOCK + r + 16)
        wr, wi, tr, ti = spec[b, re], spec[b, im], taps_spec(re), taps_spec(im)
        product[b, re] = (wr * tr - wi * ti).astype(BF16)
        product[b, im] = (wr * ti + wi * tr).astype(BF16)


def staged(fwd_of, signal_of, back, taps_spec, spec, product, blocks):
    for b in blocks:
        spec[b] = dot(fwd_of(b), signal_of(b))
    for b in blocks:
        pointwise(spec, product, taps_spec, b)
    for b in blocks:
        yield b, dot(back, product[b])


def lane_window(i, width):
    return pl.ds(pl.multiple_of(i * width, width), width)


def short_block(values, before, gate, taps, keep, window, slot, first, rows, i):
    for tile in range(WIDE // LANES):
        lanes = pl.ds(pl.multiple_of(i * WIDE + tile * LANES, LANES), LANES)
        window[slot + tile, 0:16] = before(lanes).astype(F32) * keep
        window[slot + tile, 16 : 16 + BLOCK] = values[rows, lanes].astype(F32)
        weights = taps[:, lanes].astype(F32)
        total = window[slot + tile, 16 : 16 + BLOCK] * weights[0:1]
        for k in range(1, SHORT_TAPS):
            total = total + window[slot + tile, 16 - k : 16 - k + BLOCK] * weights[k : k + 1]
        shifted = slice(rows.start + BLOCK, rows.stop + BLOCK)
        first[shifted, lanes] = (gate[rows, lanes].astype(F32) * total).astype(BF16)


def sublane_sums(stack):
    sub = lax.broadcasted_iota(jnp.int32, (8, LANES), 0)
    groups = []
    for g in range(0, MODES, 8):
        level = [stack[g + m] for m in range(8)]
        for shift in (1, 2, 4):
            low = (sub & shift) == 0
            level = [
                jnp.where(low, a, b) + pltpu.roll(jnp.where(low, b, a), shift, 0)
                for a, b in zip(level[0::2], level[1::2])
            ]
        groups.append(level[0])
    return jnp.concatenate(groups, axis=0)


def long_filter(rate_ref, residue_ref, skip_ref, fwd_ref, pair_ref, amplitude_ref, filt, long_spec, i):
    sub = lax.broadcasted_iota(jnp.int32, (1, 8, 1), 1).astype(F32)
    for tile in range(WIDE // LANES):
        own = slice(tile * LANES, (tile + 1) * LANES)
        lanes = pl.ds(pl.multiple_of(i * WIDE + tile * LANES, LANES), LANES)
        rate = rate_ref[:, lanes]
        x = 2.0 * rate
        series = x * (1.0 - x * (1 / 2) * (1.0 - x * (1 / 3) * (1.0 - x * (1 / 4) * (1.0 - x * (1 / 5)))))
        amplitude = residue_ref[:, lanes] * jnp.sqrt(jnp.where(x < 0.05, series, 1.0 - jnp.exp(-x)))
        amplitude_ref[:, lanes] = amplitude
        rate = rate[:, None, :]
        step = jnp.broadcast_to(jnp.exp(-8.0 * rate), (MODES, 8, LANES))
        part = amplitude[:, None, :] * jnp.exp(-sub * rate)
        for j in range(BLOCK // 8):
            filt[8 * j : 8 * j + 8, own] = jnp.sum(part, axis=0)
            part = part * step
        filt[0:1, own] = filt[0:1, own] + skip_ref[0:1, lanes]
    high = filt[...].astype(BF16)
    lanes = lane_window(i, WIDE)
    long_spec[:, lanes] = dot(pair_ref[...], jnp.concatenate([high, high], axis=0))


def block_states(second, rate_ref, local, blocks, i):
    sub = lax.broadcasted_iota(jnp.int32, (1, 8, 1), 1).astype(F32)
    for tile in range(WIDE // LANES):
        lanes = pl.ds(pl.multiple_of(i * WIDE + tile * LANES, LANES), LANES)
        rate = rate_ref[:, lanes][:, None, :]
        step = jnp.broadcast_to(jnp.exp(-8.0 * rate), (MODES, 8, LANES))
        weight = jnp.exp((sub - 8.0) * rate)
        for b in blocks:
            signal = second[b * BLOCK : (b + 1) * BLOCK, lanes].astype(F32)
            acc = jnp.broadcast_to(signal[0:8][None], (MODES, 8, LANES))
            for j in range(1, BLOCK // 8):
                acc = acc * step + signal[8 * j : 8 * j + 8][None]
            local[b, :, lanes] = sublane_sums(acc * weight)


def kernel_states(
    genome_ref, values_hbm, gate_one_hbm, gate_two_hbm, short_hbm, taps_ref, rate_hbm, residue_hbm, skip_hbm, fwd_hbm, pair_hbm,
    back_hbm, back_start_hbm,
    intra_out, local_out, incoming_out, amplitude_out,
    values, gate_one, gate_two, first, second, rim, taps_full, taps_spec, local, ends_own, ends, entering,
    fwd_keep, window, spec, product, amplitude, filt, long_spec, intra,
    short_ref, rate_ref, residue_ref, skip_ref, fwd_ref, pair_ref, back_ref, back_start_ref,
    small_sem, load_sem, store_sem, rim_sem, halo_send, halo_recv, taps_send, taps_recv, ends_send, ends_recv, enter_send, enter_recv, intra_sem,
):
    rows, channels = values.shape
    count = rows // BLOCK
    chunks = channels // WIDE
    parts = lax.axis_size("seq")
    width = channels // parts
    per_chunk = WIDE // width
    dps = lax.axis_size("dp")
    chips = dps // 2
    seq = lax.axis_index("seq")
    dp = lax.axis_index("dp")
    chip, core = dp // 2, dp % 2
    twin = chip * 2 + (1 - core)
    following = lax.rem(seq + 1, parts)
    keeps = keep_scalars(genome_ref, seq, count)
    tail = rows - BLOCK

    def remote(src, dst, send, recv, dp_to, seq_to):
        return pltpu.make_async_remote_copy(
            src_ref=src, dst_ref=dst, send_sem=send, recv_sem=recv,
            device_id=(dp_to, seq_to), device_id_type=pl.DeviceIdType.MESH,
        )

    loads = []
    for src, dst, part in (
        (values_hbm, values, slice(tail - 16, rows)),
        (gate_one_hbm, gate_one, slice(tail, rows)),
        (values_hbm, values, slice(0, tail - 16)),
        (gate_one_hbm, gate_one, slice(0, tail)),
        (gate_two_hbm, gate_two, slice(0, rows)),
    ):
        loads.append(pltpu.make_async_copy(src.at[part], dst.at[part], load_sem.at[len(loads)]))
    small = [
        pltpu.make_async_copy(src, dst, small_sem.at[n])
        for n, (src, dst) in enumerate(
            (
                (short_hbm, short_ref), (fwd_hbm, fwd_ref), (rate_hbm, rate_ref), (residue_hbm, residue_ref),
                (skip_hbm, skip_ref), (pair_hbm, pair_ref), (back_hbm, back_ref), (back_start_hbm, back_start_ref),
            )
        )
    ]
    small[0].start()
    loads[0].start()
    loads[1].start()
    for copy in small[1:]:
        copy.start()

    barrier = pltpu.get_barrier_semaphore()
    peers = 0
    for k in range(1, parts):
        pl.semaphore_signal(
            barrier, inc=1, device_id=(dp, lax.rem(seq + k, parts)), device_id_type=pl.DeviceIdType.MESH
        )
        peers += 1
    for k in range(1, chips):
        pl.semaphore_signal(
            barrier, inc=1, device_id=(lax.rem(chip + k, chips) * 2 + core, seq), device_id_type=pl.DeviceIdType.MESH
        )
        peers += 1
    pl.semaphore_signal(barrier, inc=1, device_id=(twin, seq), device_id_type=pl.DeviceIdType.MESH)
    pl.semaphore_wait(barrier, peers + 1)

    rim_copy = remote(values_hbm.at[slice(rows - 16, rows)], rim, rim_sem.at[0], rim_sem.at[1], dp, following)
    rim_copy.start()

    def taps_copy(slot, index, src, dp_to):
        return remote(src, taps_full.at[slot], taps_send.at[index], taps_recv.at[slot], dp_to, seq)

    taps_own = pltpu.make_async_copy(taps_ref, taps_full.at[dp], taps_recv.at[dp])
    taps_own.start()
    taps_copies = [taps_copy(dp, k - 1, taps_ref, lax.rem(chip + k, chips) * 2 + core) for k in range(1, chips)]
    taps_copies.append(taps_copy(dp, chips - 1, taps_ref, twin))
    for copy in taps_copies:
        copy.start()

    loads[0].wait()
    loads[1].wait()
    small[0].wait()
    for copy in loads[2:]:
        copy.start()

    def halo_copy(i):
        lanes = lane_window(i, WIDE)
        return remote(
            first.at[slice(rows, rows + BLOCK), lanes], first.at[slice(0, BLOCK), lanes], halo_send.at[i], halo_recv.at[i], dp, following
        )

    def tail_step(i, carry):
        short_block(
            values, lambda lanes: values[tail - 16 : tail, lanes], gate_one, short_ref, keeps[count - 1], window, 0, first,
            slice(tail, rows), i,
        )
        halo_copy(i).start()
        return carry

    lax.fori_loop(0, chunks, tail_step, 0)

    for copy in small[1:]:
        copy.wait()
    for b in range(count):
        column = lax.broadcasted_iota(jnp.int32, fwd_ref.shape, 1)
        matrix = fwd_ref[...].astype(F32)
        fwd_keep[b] = jnp.where(column < BLOCK, matrix * keeps[b], matrix).astype(BF16)

    def filter_step(i, carry):
        long_filter(rate_ref, residue_ref, skip_ref, fwd_ref, pair_ref, amplitude, filt, long_spec, i)
        return carry

    lax.fori_loop(0, chunks * 3 // 4, filter_step, 0)

    loads[2].wait()
    loads[3].wait()
    rim_copy.wait()

    def first_step(i, carry):
        for b in range(count - 1):
            start = b * BLOCK
            if b == 0:
                before = lambda lanes: rim[:, lanes]
            else:
                before = lambda lanes, start=start: values[start - 16 : start, lanes]
            short_block(
                values, before, gate_one, short_ref, keeps[b], window, b * (WIDE // LANES), first, slice(start, start + BLOCK), i
            )
        return carry

    lax.fori_loop(0, chunks, first_step, 0)

    forwards = []
    for k in range(1, chips):
        source = lax.rem(chip + k, chips) * 2 + core
        taps_copy(source, k - 1, taps_ref, source).wait_recv()
        copy = taps_copy(source, chips - 1 + k, taps_full.at[source], twin)
        copy.start()
        forwards.append(copy)
    taps_own.wait()
    for k in range(chips):
        source = lax.rem(chip + k, chips) * 2 + (1 - core)
        taps_copy(source, chips - 1, taps_ref, twin).wait_recv()
    loads[4].wait()

    def second_step(i, carry):
        lanes = lane_window(i, WIDE)
        taps = taps_full[i]
        taps_spec[:, lanes] = dot(pair_ref[...], jnp.concatenate([taps, taps], axis=0))
        blocks = range(1, count)
        for b, medium in staged(
            lambda b: fwd_keep[b], lambda b: first[b * BLOCK : (b + 2) * BLOCK, lanes], back_ref[...],
            lambda part: taps_spec[part, lanes], spec, product, blocks,
        ):
            part = slice(b * BLOCK, (b + 1) * BLOCK)
            second[part, lanes] = (gate_two[part, lanes].astype(F32) * medium).astype(BF16)
        block_states(second, rate_ref, local, blocks, i)
        return carry

    lax.fori_loop(0, chunks, second_step, 0)
    def ends_copy(part):
        return remote(ends_own.at[part], ends.at[seq], ends_send.at[part], ends_recv.at[seq], dp, part)

    def opening_step(pair, carry):
        both = [pair * 4 + n for n in range(4)]
        for h, i in enumerate(both):
            halo_copy(i).wait_recv()
        for h, i in enumerate(both):
            lanes = lane_window(i, WIDE)
            spec[h] = dot(fwd_keep[0], first[0 : 2 * BLOCK, lanes])
        for h, i in enumerate(both):
            lanes = lane_window(i, WIDE)
            pointwise(spec, product, lambda part: taps_spec[part, lanes], h)
        for h, i in enumerate(both):
            lanes = lane_window(i, WIDE)
            medium = dot(back_ref[...], product[h])
            second[0:BLOCK, lanes] = (gate_two[0:BLOCK, lanes].astype(F32) * medium).astype(BF16)
        for i in both:
            lanes = lane_window(i, WIDE)
            block_states(second, rate_ref, local, range(1), i)
            decay = jnp.exp(-float(BLOCK) * rate_ref[:, lanes])
            total = local[0, :, lanes]
            for b in range(1, count):
                total = keeps[b] * decay * total + local[b, :, lanes]
            for h in range(per_chunk):
                part = i * per_chunk + h
                ends_own[part] = total[:, h * width : (h + 1) * width]

                @pl.when(part != seq)
                def _():
                    ends_copy(part).start()

                @pl.when(part == seq)
                def _():
                    ends[part] = total[:, h * width : (h + 1) * width]

        return carry

    lax.fori_loop(0, chunks // 4, opening_step, 0)
    store_local = pltpu.make_async_copy(local, local_out, store_sem.at[1])
    store_local.start()

    def intra_copy(i):
        lanes = lane_window(i, WIDE)
        return pltpu.make_async_copy(intra.at[:, lanes], intra_out.at[:, lanes], intra_sem.at[i])

    def intra_step(i, carry):
        lanes = lane_window(i, WIDE)
        for b, result in staged(
            lambda b: fwd_ref[:, :BLOCK], lambda b: second[b * BLOCK : (b + 1) * BLOCK, lanes], back_start_ref[...],
            lambda part: long_spec[part, lanes], spec, product, range(count),
        ):
            intra[b * BLOCK : (b + 1) * BLOCK, lanes] = result.astype(INTRA)
        intra_copy(i).start()
        return carry

    lax.fori_loop(0, chunks // 2, intra_step, 0)

    def arrival(k, carry):
        source = lax.rem(seq + k, parts)
        remote(ends_own.at[source], ends.at[source], ends_send.at[source], ends_recv.at[source], dp, source).wait_recv()
        return carry

    lax.fori_loop(1, parts, arrival, 0)

    begins = [jnp.int32(0)]
    for g in range(genome_ref.shape[1] - 1):
        begins.append(begins[-1] + genome_ref[0, g])
    decay = jnp.exp(-float(rows) * rate_ref[:, lane_window(seq, width)])

    def enter_copy(p):
        return remote(entering.at[p], incoming_out.at[seq], enter_send.at[p], enter_recv.at[seq], dp, p)

    def scan_step(p, state):
        entering[p] = state

        @pl.when(p != seq)
        def _():
            enter_copy(p).start()

        through = jnp.float32(1.0)
        for b in range(count):
            for begin in begins:
                through = jnp.where(p * count + b == begin, 0.0, through)
        return through * decay * state + ends[p]

    lax.fori_loop(0, parts, scan_step, jnp.zeros((MODES, width), F32))
    lax.fori_loop(chunks * 3 // 4, chunks, filter_step, 0)
    store_amplitude = pltpu.make_async_copy(amplitude, amplitude_out, store_sem.at[0])
    store_amplitude.start()
    lax.fori_loop(chunks // 2, chunks, intra_step, 0)
    enter_own = pltpu.make_async_copy(entering.at[seq], incoming_out.at[seq], store_sem.at[2])
    enter_own.start()

    def departures(k, carry):
        other = lax.rem(seq + k, parts)
        ends_copy(other).wait_send()
        enter_copy(other).wait_send()
        remote(entering.at[other], incoming_out.at[other], enter_send.at[other], enter_recv.at[other], dp, other).wait_recv()
        return carry

    lax.fori_loop(1, parts, departures, 0)

    def halo_sent(i, carry):
        halo_copy(i).wait_send()
        intra_copy(i).wait()
        return carry

    lax.fori_loop(0, chunks, halo_sent, 0)
    for copy in taps_copies + forwards:
        copy.wait_send()
    for copy in (store_amplitude, store_local, enter_own):
        copy.wait()


def kernel_mixed(genome_ref, intra_ref, gate_ref, local_ref, incoming_ref, rate_ref, amplitude_ref, mixed_ref):
    count = intra_ref.shape[0] // BLOCK
    keeps = keep_scalars(genome_ref, lax.axis_index("seq"), count)
    sub = lax.broadcasted_iota(jnp.int32, (1, 8, 1), 1).astype(F32)
    width = incoming_ref.shape[2]
    for tile in range(WIDE // LANES):
        lanes = slice(tile * LANES, (tile + 1) * LANES)
        rate = rate_ref[:, lanes]
        decay = jnp.exp(-float(BLOCK) * rate)
        rate = rate[:, None, :]
        step = jnp.broadcast_to(jnp.exp(-8.0 * rate), (MODES, 8, LANES))
        weight = amplitude_ref[:, lanes][:, None, :] * jnp.exp(-sub * rate)
        piece, offset = tile * LANES // width, tile * LANES % width
        state = incoming_ref[piece, :, offset : offset + LANES]
        for b in range(count):
            state = state * keeps[b]
            part = weight * state[:, None, :]
            for j in range(0, BLOCK, 16):
                rows = slice(b * BLOCK + j, b * BLOCK + j + 16)
                upper = jnp.sum(part, axis=0)
                part = part * step
                lower = jnp.sum(part, axis=0)
                part = part * step
                total = intra_ref[rows, lanes].astype(F32) + jnp.concatenate([upper, lower], axis=0)
                mixed_ref[rows, lanes] = (gate_ref[rows, lanes].astype(F32) * total).astype(BF16)
            if b < count - 1:
                state = decay * state + local_ref[b, :, lanes]


def chunked(rows):
    return pl.BlockSpec((rows, WIDE), lambda i: (0, i))


def whole(shape):
    return pl.BlockSpec(shape, lambda i: (0,) * len(shape))


def body(values, gate_one, gate_two, gate_three, genome_blocks, short_taps, medium_taps, decay_rate, residue, long_skip):
    rows, channels = values.shape[1:]
    count = rows // BLOCK
    parts = lax.axis_size("seq")
    dps = lax.axis_size("dp")
    width = channels // parts
    chunks = channels // WIDE
    fwd, pair, back_end, back_start = [jnp.asarray(m) for m in transform_matrices()]
    rate = decay_rate.T
    smem = pl.BlockSpec(memory_space=pltpu.SMEM)
    hbm = pl.BlockSpec(memory_space=pl.ANY)
    stream = pltpu.VMEM((rows, channels), BF16)
    dma = pltpu.SemaphoreType.DMA

    intra, local, incoming, amplitude = pl.pallas_call(
        kernel_states,
        in_specs=[smem] + [hbm] * 12,
        out_specs=[hbm] * 4,
        out_shape=[
            jax.ShapeDtypeStruct((rows, channels), INTRA),
            jax.ShapeDtypeStruct((count, MODES, channels), F32),
            jax.ShapeDtypeStruct((parts, MODES, width), F32),
            jax.ShapeDtypeStruct((MODES, channels), F32),
        ],
        scratch_shapes=[
            stream, stream, stream,
            pltpu.VMEM((rows + BLOCK, channels), BF16),
            stream,
            pltpu.VMEM((16, channels), BF16),
            pltpu.VMEM((dps, BLOCK, WIDE), BF16),
            pltpu.VMEM((2 * BLOCK, channels), F32),
            pltpu.VMEM((count, MODES, channels), F32),
            pltpu.VMEM((parts, MODES, width), F32),
            pltpu.VMEM((parts, MODES, width), F32),
            pltpu.VMEM((parts, MODES, width), F32),
            pltpu.VMEM((count, 2 * BLOCK, 2 * BLOCK), BF16),
            pltpu.VMEM((count * (WIDE // LANES), 16 + BLOCK, LANES), F32),
            pltpu.VMEM((count, 2 * BLOCK, WIDE), F32),
            pltpu.VMEM((count, 2 * BLOCK, WIDE), BF16),
            pltpu.VMEM((MODES, channels), F32),
            pltpu.VMEM((BLOCK, WIDE), F32),
            pltpu.VMEM((2 * BLOCK, channels), F32),
            pltpu.VMEM((rows, channels), INTRA),
            pltpu.VMEM((SHORT_TAPS, channels), BF16),
            pltpu.VMEM((MODES, channels), F32),
            pltpu.VMEM((MODES, channels), F32),
            pltpu.VMEM((1, channels), F32),
            pltpu.VMEM(fwd.shape, BF16),
            pltpu.VMEM(pair.shape, BF16),
            pltpu.VMEM(back_end.shape, BF16),
            pltpu.VMEM(back_start.shape, BF16),
            dma((8,)), dma((5,)), dma((3,)), dma((2,)), dma((chunks,)), dma((chunks,)), dma((dps,)), dma((dps,)),
            dma((parts,)), dma((parts,)), dma((parts,)), dma((parts,)), dma((chunks,)),
        ],
        compiler_params=pltpu.CompilerParams(
            vmem_limit_bytes=VMEM_LIMIT, collective_id=0, has_side_effects=True
        ),
        name="states",
    )(
        genome_blocks, values[0], gate_one[0], gate_two[0], short_taps, medium_taps, rate, residue.T, long_skip[None],
        fwd, pair, back_end, back_start,
    )

    per_chunk = WIDE // width
    mixed = pl.pallas_call(
        kernel_mixed,
        grid=(chunks,),
        in_specs=[
            smem, chunked(rows), chunked(rows), pl.BlockSpec((count, MODES, WIDE), lambda i: (0, 0, i)),
            pl.BlockSpec((per_chunk, MODES, width), lambda i: (i, 0, 0)),
            chunked(MODES), chunked(MODES),
        ],
        out_specs=chunked(rows),
        out_shape=jax.ShapeDtypeStruct((rows, channels), BF16),
        compiler_params=pltpu.CompilerParams(vmem_limit_bytes=VMEM_LIMIT),
        name="mixed",
    )(genome_blocks, intra, gate_three[0], local, incoming, rate, amplitude)
    return mixed[None]


def solution(mesh):
    return jax.shard_map(
        body,
        mesh=mesh,
        in_specs=(
            P("dp", "seq", None),
            P("dp", "seq", None),
            P("dp", "seq", None),
            P("dp", "seq", None),
            P("dp", None),
            P(),
            P(None, "dp"),
            P(),
            P(),
            P(),
        ),
        out_specs=P("dp", "seq", None),
        check_vma=False,
    )
```

```python
import functools

import jax
import jax.numpy as jnp
import numpy as np
from jax import lax
from jax.experimental import pallas as pl
from jax.experimental.pallas import tpu as pltpu
from jax.sharding import PartitionSpec as P

SHORT_TAPS = 7
MED_TAPS = 128
BLOCK = 128
WIDE = 512
MODES = 16
LANES = 128
F32 = jnp.float32
BF16 = jnp.bfloat16
INTRA = BF16
VMEM_LIMIT = 58 * 1024 * 1024


def transform_matrices():
    n = np.arange(2 * BLOCK)
    j = np.arange(BLOCK)
    angle = np.pi * (2 * j + 1)[:, None] * n[None] / (2 * BLOCK)
    forward = np.concatenate([np.cos(angle), -np.sin(angle)], axis=0)
    backward = np.concatenate([np.cos(angle).T, -np.sin(angle).T], axis=1) / BLOCK
    high = forward.astype(jnp.bfloat16)
    low = (forward - high.astype(np.float64)).astype(jnp.bfloat16)
    return high, np.concatenate([high[:, :BLOCK], low[:, :BLOCK]], axis=1), backward[BLOCK:].astype(jnp.bfloat16), backward[:BLOCK].astype(jnp.bfloat16)


def keep_scalars(genome_ref, position, count):
    begins = [jnp.int32(0)]
    for g in range(genome_ref.shape[1] - 1):
        begins.append(begins[-1] + genome_ref[0, g])
    keeps = []
    for b in range(count):
        block = position * count + b
        starts = functools.reduce(jnp.logical_or, [block == begin for begin in begins])
        keeps.append(jnp.where(starts, 0.0, 1.0).astype(F32))
    return keeps


def dot(a, b):
    return jnp.dot(a, b, preferred_element_type=F32)


def pointwise(spec, product, taps_spec, b):
    for r in range(0, BLOCK, 16):
        re, im = slice(r, r + 16), slice(BLOCK + r, BLOCK + r + 16)
        wr, wi, tr, ti = spec[b, re], spec[b, im], taps_spec(re), taps_spec(im)
        product[b, re] = (wr * tr - wi * ti).astype(BF16)
        product[b, im] = (wr * ti + wi * tr).astype(BF16)


def staged(fwd_of, signal_of, back, taps_spec, spec, product, blocks):
    for b in blocks:
        spec[b] = dot(fwd_of(b), signal_of(b))
    for b in blocks:
        pointwise(spec, product, taps_spec, b)
    for b in blocks:
        yield b, dot(back, product[b])


def lane_window(i, width):
    return pl.ds(pl.multiple_of(i * width, width), width)


def short_block(values, before, gate, taps, keep, window, slot, first, rows, i):
    for tile in range(WIDE // LANES):
        lanes = pl.ds(pl.multiple_of(i * WIDE + tile * LANES, LANES), LANES)
        window[slot + tile, 0:16] = before(lanes).astype(F32) * keep
        window[slot + tile, 16 : 16 + BLOCK] = values[rows, lanes].astype(F32)
        weights = taps[:, lanes].astype(F32)
        total = window[slot + tile, 16 : 16 + BLOCK] * weights[0:1]
        for k in range(1, SHORT_TAPS):
            total = total + window[slot + tile, 16 - k : 16 - k + BLOCK] * weights[k : k + 1]
        shifted = slice(rows.start + BLOCK, rows.stop + BLOCK)
        first[shifted, lanes] = (gate[rows, lanes].astype(F32) * total).astype(BF16)


def sublane_sums(stack):
    sub = lax.broadcasted_iota(jnp.int32, (8, LANES), 0)
    groups = []
    for g in range(0, MODES, 8):
        level = [stack[g + m] for m in range(8)]
        for shift in (1, 2, 4):
            low = (sub & shift) == 0
            level = [
                jnp.where(low, a, b) + pltpu.roll(jnp.where(low, b, a), shift, 0)
                for a, b in zip(level[0::2], level[1::2])
            ]
        groups.append(level[0])
    return jnp.concatenate(groups, axis=0)


def long_filter(rate_ref, residue_ref, skip_ref, fwd_ref, pair_ref, amplitude_ref, filt, long_spec, i):
    sub = lax.broadcasted_iota(jnp.int32, (1, 8, 1), 1).astype(F32)
    for tile in range(WIDE // LANES):
        own = slice(tile * LANES, (tile + 1) * LANES)
        lanes = pl.ds(pl.multiple_of(i * WIDE + tile * LANES, LANES), LANES)
        rate = rate_ref[:, lanes]
        x = 2.0 * rate
        series = x * (1.0 - x * (1 / 2) * (1.0 - x * (1 / 3) * (1.0 - x * (1 / 4) * (1.0 - x * (1 / 5)))))
        amplitude = residue_ref[:, lanes] * jnp.sqrt(jnp.where(x < 0.05, series, 1.0 - jnp.exp(-x)))
        amplitude_ref[:, lanes] = amplitude
        rate = rate[:, None, :]
        step = jnp.broadcast_to(jnp.exp(-8.0 * rate), (MODES, 8, LANES))
        part = amplitude[:, None, :] * jnp.exp(-sub * rate)
        for j in range(BLOCK // 8):
            filt[8 * j : 8 * j + 8, own] = jnp.sum(part, axis=0)
            part = part * step
        filt[0:1, own] = filt[0:1, own] + skip_ref[0:1, lanes]
    high = filt[...].astype(BF16)
    lanes = lane_window(i, WIDE)
    long_spec[:, lanes] = dot(pair_ref[...], jnp.concatenate([high, high], axis=0))


def block_states(second, rate_ref, local, blocks, i):
    sub = lax.broadcasted_iota(jnp.int32, (1, 8, 1), 1).astype(F32)
    for tile in range(WIDE // LANES):
        lanes = pl.ds(pl.multiple_of(i * WIDE + tile * LANES, LANES), LANES)
        rate = rate_ref[:, lanes][:, None, :]
        step = jnp.broadcast_to(jnp.exp(-8.0 * rate), (MODES, 8, LANES))
        weight = jnp.exp((sub - 8.0) * rate)
        for b in blocks:
            signal = second[b * BLOCK : (b + 1) * BLOCK, lanes].astype(F32)
            acc = jnp.broadcast_to(signal[0:8][None], (MODES, 8, LANES))
            for j in range(1, BLOCK // 8):
                acc = acc * step + signal[8 * j : 8 * j + 8][None]
            local[b, :, lanes] = sublane_sums(acc * weight)


def kernel_states(
    genome_ref, values_hbm, gate_one_hbm, gate_two_hbm, short_hbm, taps_ref, rate_hbm, residue_hbm, skip_hbm, fwd_hbm, pair_hbm,
    back_hbm, back_start_hbm,
    intra_out, local_out, incoming_out, amplitude_out,
    values, gate_one, gate_two, first, second, rim, taps_full, taps_spec, local, ends_own, ends, entering,
    fwd_keep, window, spec, product, amplitude, filt, long_spec, intra,
    short_ref, rate_ref, residue_ref, skip_ref, fwd_ref, pair_ref, back_ref, back_start_ref,
    small_sem, load_sem, store_sem, rim_sem, halo_send, halo_recv, taps_send, taps_recv, ends_send, ends_recv, enter_send, enter_recv, intra_sem,
):
    rows, channels = values.shape
    count = rows // BLOCK
    chunks = channels // WIDE
    parts = lax.axis_size("seq")
    width = channels // parts
    per_chunk = WIDE // width
    dps = lax.axis_size("dp")
    chips = dps // 2
    seq = lax.axis_index("seq")
    dp = lax.axis_index("dp")
    chip, core = dp // 2, dp % 2
    twin = chip * 2 + (1 - core)
    following = lax.rem(seq + 1, parts)
    keeps = keep_scalars(genome_ref, seq, count)
    tail = rows - BLOCK

    def remote(src, dst, send, recv, dp_to, seq_to):
        return pltpu.make_async_remote_copy(
            src_ref=src, dst_ref=dst, send_sem=send, recv_sem=recv,
            device_id=(dp_to, seq_to), device_id_type=pl.DeviceIdType.MESH,
        )

    loads = []
    for src, dst, part in (
        (values_hbm, values, slice(tail - 16, rows)),
        (gate_one_hbm, gate_one, slice(tail, rows)),
        (values_hbm, values, slice(0, tail - 16)),
        (gate_one_hbm, gate_one, slice(0, tail)),
        (gate_two_hbm, gate_two, slice(0, rows)),
    ):
        loads.append(pltpu.make_async_copy(src.at[part], dst.at[part], load_sem.at[len(loads)]))
    small = [
        pltpu.make_async_copy(src, dst, small_sem.at[n])
        for n, (src, dst) in enumerate(
            (
                (short_hbm, short_ref), (fwd_hbm, fwd_ref), (rate_hbm, rate_ref), (residue_hbm, residue_ref),
                (skip_hbm, skip_ref), (pair_hbm, pair_ref), (back_hbm, back_ref), (back_start_hbm, back_start_ref),
            )
        )
    ]
    small[0].start()
    loads[0].start()
    loads[1].start()
    for copy in small[1:]:
        copy.start()

    barrier = pltpu.get_barrier_semaphore()
    peers = 0
    for k in range(1, parts):
        pl.semaphore_signal(
            barrier, inc=1, device_id=(dp, lax.rem(seq + k, parts)), device_id_type=pl.DeviceIdType.MESH
        )
        peers += 1
    for k in range(1, chips):
        pl.semaphore_signal(
            barrier, inc=1, device_id=(lax.rem(chip + k, chips) * 2 + core, seq), device_id_type=pl.DeviceIdType.MESH
        )
        peers += 1
    pl.semaphore_signal(barrier, inc=1, device_id=(twin, seq), device_id_type=pl.DeviceIdType.MESH)
    pl.semaphore_wait(barrier, peers + 1)

    rim_copy = remote(values_hbm.at[slice(rows - 16, rows)], rim, rim_sem.at[0], rim_sem.at[1], dp, following)
    rim_copy.start()

    def taps_copy(slot, index, src, dp_to):
        return remote(src, taps_full.at[slot], taps_send.at[index], taps_recv.at[slot], dp_to, seq)

    taps_own = pltpu.make_async_copy(taps_ref, taps_full.at[dp], taps_recv.at[dp])
    taps_own.start()
    taps_copies = [taps_copy(dp, k - 1, taps_ref, lax.rem(chip + k, chips) * 2 + core) for k in range(1, chips)]
    taps_copies.append(taps_copy(dp, chips - 1, taps_ref, twin))
    for copy in taps_copies:
        copy.start()

    loads[0].wait()
    loads[1].wait()
    small[0].wait()
    for copy in loads[2:]:
        copy.start()

    def halo_copy(i):
        lanes = lane_window(i, WIDE)
        return remote(
            first.at[slice(rows, rows + BLOCK), lanes], first.at[slice(0, BLOCK), lanes], halo_send.at[i], halo_recv.at[i], dp, following
        )

    def tail_step(i, carry):
        short_block(
            values, lambda lanes: values[tail - 16 : tail, lanes], gate_one, short_ref, keeps[count - 1], window, 0, first,
            slice(tail, rows), i,
        )
        halo_copy(i).start()
        return carry

    lax.fori_loop(0, chunks, tail_step, 0)

    for copy in small[1:]:
        copy.wait()
    for b in range(count):
        column = lax.broadcasted_iota(jnp.int32, fwd_ref.shape, 1)
        matrix = fwd_ref[...].astype(F32)
        fwd_keep[b] = jnp.where(column < BLOCK, matrix * keeps[b], matrix).astype(BF16)

    def filter_step(i, carry):
        long_filter(rate_ref, residue_ref, skip_ref, fwd_ref, pair_ref, amplitude, filt, long_spec, i)
        return carry

    lax.fori_loop(0, chunks, filter_step, 0)

    loads[2].wait()
    loads[3].wait()
    rim_copy.wait()

    def first_step(i, carry):
        for b in range(count - 1):
            start = b * BLOCK
            if b == 0:
                before = lambda lanes: rim[:, lanes]
            else:
                before = lambda lanes, start=start: values[start - 16 : start, lanes]
            short_block(
                values, before, gate_one, short_ref, keeps[b], window, b * (WIDE // LANES), first, slice(start, start + BLOCK), i
            )
        return carry

    lax.fori_loop(0, chunks, first_step, 0)

    forwards = []
    for k in range(1, chips):
        source = lax.rem(chip + k, chips) * 2 + core
        taps_copy(source, k - 1, taps_ref, source).wait_recv()
        copy = taps_copy(source, chips - 1 + k, taps_full.at[source], twin)
        copy.start()
        forwards.append(copy)
    taps_own.wait()
    for k in range(chips):
        source = lax.rem(chip + k, chips) * 2 + (1 - core)
        taps_copy(source, chips - 1, taps_ref, twin).wait_recv()
    loads[4].wait()

    def second_step(i, carry):
        lanes = lane_window(i, WIDE)
        taps = taps_full[i]
        taps_spec[:, lanes] = dot(pair_ref[...], jnp.concatenate([taps, taps], axis=0))
        blocks = range(1, count)
        for b, medium in staged(
            lambda b: fwd_keep[b], lambda b: first[b * BLOCK : (b + 2) * BLOCK, lanes], back_ref[...],
            lambda part: taps_spec[part, lanes], spec, product, blocks,
        ):
            part = slice(b * BLOCK, (b + 1) * BLOCK)
            second[part, lanes] = (gate_two[part, lanes].astype(F32) * medium).astype(BF16)
        block_states(second, rate_ref, local, blocks, i)
        return carry

    lax.fori_loop(0, chunks, second_step, 0)
    def ends_copy(part):
        return remote(ends_own.at[part], ends.at[seq], ends_send.at[part], ends_recv.at[seq], dp, part)

    def opening_step(pair, carry):
        both = [pair * 4 + n for n in range(4)]
        for h, i in enumerate(both):
            halo_copy(i).wait_recv()
        for h, i in enumerate(both):
            lanes = lane_window(i, WIDE)
            spec[h] = dot(fwd_keep[0], first[0 : 2 * BLOCK, lanes])
        for h, i in enumerate(both):
            lanes = lane_window(i, WIDE)
            pointwise(spec, product, lambda part: taps_spec[part, lanes], h)
        for h, i in enumerate(both):
            lanes = lane_window(i, WIDE)
            medium = dot(back_ref[...], product[h])
            second[0:BLOCK, lanes] = (gate_two[0:BLOCK, lanes].astype(F32) * medium).astype(BF16)
        for i in both:
            lanes = lane_window(i, WIDE)
            block_states(second, rate_ref, local, range(1), i)
            decay = jnp.exp(-float(BLOCK) * rate_ref[:, lanes])
            total = local[0, :, lanes]
            for b in range(1, count):
                total = keeps[b] * decay * total + local[b, :, lanes]
            for h in range(per_chunk):
                part = i * per_chunk + h
                ends_own[part] = total[:, h * width : (h + 1) * width]

                @pl.when(part != seq)
                def _():
                    ends_copy(part).start()

                @pl.when(part == seq)
                def _():
                    ends[part] = total[:, h * width : (h + 1) * width]

        return carry

    lax.fori_loop(0, chunks // 4, opening_step, 0)
    store_local = pltpu.make_async_copy(local, local_out, store_sem.at[1])
    store_local.start()

    def intra_copy(i):
        lanes = lane_window(i, WIDE)
        return pltpu.make_async_copy(intra.at[:, lanes], intra_out.at[:, lanes], intra_sem.at[i])

    def intra_step(i, carry):
        lanes = lane_window(i, WIDE)
        for b, result in staged(
            lambda b: fwd_ref[:, :BLOCK], lambda b: second[b * BLOCK : (b + 1) * BLOCK, lanes], back_start_ref[...],
            lambda part: long_spec[part, lanes], spec, product, range(count),
        ):
            intra[b * BLOCK : (b + 1) * BLOCK, lanes] = result.astype(INTRA)
        intra_copy(i).start()
        return carry

    lax.fori_loop(0, chunks // 2, intra_step, 0)

    def arrival(k, carry):
        source = lax.rem(seq + k, parts)
        remote(ends_own.at[source], ends.at[source], ends_send.at[source], ends_recv.at[source], dp, source).wait_recv()
        return carry

    lax.fori_loop(1, parts, arrival, 0)

    begins = [jnp.int32(0)]
    for g in range(genome_ref.shape[1] - 1):
        begins.append(begins[-1] + genome_ref[0, g])
    decay = jnp.exp(-float(rows) * rate_ref[:, lane_window(seq, width)])

    def enter_copy(p):
        return remote(entering.at[p], incoming_out.at[seq], enter_send.at[p], enter_recv.at[seq], dp, p)

    def scan_step(p, state):
        entering[p] = state

        @pl.when(p != seq)
        def _():
            enter_copy(p).start()

        through = jnp.float32(1.0)
        for b in range(count):
            for begin in begins:
                through = jnp.where(p * count + b == begin, 0.0, through)
        return through * decay * state + ends[p]

    lax.fori_loop(0, parts, scan_step, jnp.zeros((MODES, width), F32))
    store_amplitude = pltpu.make_async_copy(amplitude, amplitude_out, store_sem.at[0])
    store_amplitude.start()
    lax.fori_loop(chunks // 2, chunks, intra_step, 0)
    enter_own = pltpu.make_async_copy(entering.at[seq], incoming_out.at[seq], store_sem.at[2])
    enter_own.start()

    def departures(k, carry):
        other = lax.rem(seq + k, parts)
        ends_copy(other).wait_send()
        enter_copy(other).wait_send()
        remote(entering.at[other], incoming_out.at[other], enter_send.at[other], enter_recv.at[other], dp, other).wait_recv()
        return carry

    lax.fori_loop(1, parts, departures, 0)

    def halo_sent(i, carry):
        halo_copy(i).wait_send()
        intra_copy(i).wait()
        return carry

    lax.fori_loop(0, chunks, halo_sent, 0)
    for copy in taps_copies + forwards:
        copy.wait_send()
    for copy in (store_amplitude, store_local, enter_own):
        copy.wait()


def kernel_mixed(genome_ref, intra_ref, gate_ref, local_ref, incoming_ref, rate_ref, amplitude_ref, mixed_ref):
    count = intra_ref.shape[0] // BLOCK
    keeps = keep_scalars(genome_ref, lax.axis_index("seq"), count)
    sub = lax.broadcasted_iota(jnp.int32, (1, 8, 1), 1).astype(F32)
    width = incoming_ref.shape[2]
    for tile in range(WIDE // LANES):
        lanes = slice(tile * LANES, (tile + 1) * LANES)
        rate = rate_ref[:, lanes]
        decay = jnp.exp(-float(BLOCK) * rate)
        rate = rate[:, None, :]
        step = jnp.broadcast_to(jnp.exp(-8.0 * rate), (MODES, 8, LANES))
        weight = amplitude_ref[:, lanes][:, None, :] * jnp.exp(-sub * rate)
        piece, offset = tile * LANES // width, tile * LANES % width
        state = incoming_ref[piece, :, offset : offset + LANES]
        for b in range(count):
            state = state * keeps[b]
            part = weight * state[:, None, :]
            for j in range(0, BLOCK, 16):
                rows = slice(b * BLOCK + j, b * BLOCK + j + 16)
                upper = jnp.sum(part, axis=0)
                part = part * step
                lower = jnp.sum(part, axis=0)
                part = part * step
                total = intra_ref[rows, lanes].astype(F32) + jnp.concatenate([upper, lower], axis=0)
                mixed_ref[rows, lanes] = (gate_ref[rows, lanes].astype(F32) * total).astype(BF16)
            if b < count - 1:
                state = decay * state + local_ref[b, :, lanes]


def chunked(rows):
    return pl.BlockSpec((rows, WIDE), lambda i: (0, i))


def whole(shape):
    return pl.BlockSpec(shape, lambda i: (0,) * len(shape))


def body(values, gate_one, gate_two, gate_three, genome_blocks, short_taps, medium_taps, decay_rate, residue, long_skip):
    rows, channels = values.shape[1:]
    count = rows // BLOCK
    parts = lax.axis_size("seq")
    dps = lax.axis_size("dp")
    width = channels // parts
    chunks = channels // WIDE
    fwd, pair, back_end, back_start = [jnp.asarray(m) for m in transform_matrices()]
    rate = decay_rate.T
    smem = pl.BlockSpec(memory_space=pltpu.SMEM)
    hbm = pl.BlockSpec(memory_space=pl.ANY)
    stream = pltpu.VMEM((rows, channels), BF16)
    dma = pltpu.SemaphoreType.DMA

    intra, local, incoming, amplitude = pl.pallas_call(
        kernel_states,
        in_specs=[smem] + [hbm] * 12,
        out_specs=[hbm] * 4,
        out_shape=[
            jax.ShapeDtypeStruct((rows, channels), INTRA),
            jax.ShapeDtypeStruct((count, MODES, channels), F32),
            jax.ShapeDtypeStruct((parts, MODES, width), F32),
            jax.ShapeDtypeStruct((MODES, channels), F32),
        ],
        scratch_shapes=[
            stream, stream, stream,
            pltpu.VMEM((rows + BLOCK, channels), BF16),
            stream,
            pltpu.VMEM((16, channels), BF16),
            pltpu.VMEM((dps, BLOCK, WIDE), BF16),
            pltpu.VMEM((2 * BLOCK, channels), F32),
            pltpu.VMEM((count, MODES, channels), F32),
            pltpu.VMEM((parts, MODES, width), F32),
            pltpu.VMEM((parts, MODES, width), F32),
            pltpu.VMEM((parts, MODES, width), F32),
            pltpu.VMEM((count, 2 * BLOCK, 2 * BLOCK), BF16),
            pltpu.VMEM((count * (WIDE // LANES), 16 + BLOCK, LANES), F32),
            pltpu.VMEM((count, 2 * BLOCK, WIDE), F32),
            pltpu.VMEM((count, 2 * BLOCK, WIDE), BF16),
            pltpu.VMEM((MODES, channels), F32),
            pltpu.VMEM((BLOCK, WIDE), F32),
            pltpu.VMEM((2 * BLOCK, channels), F32),
            pltpu.VMEM((rows, channels), INTRA),
            pltpu.VMEM((SHORT_TAPS, channels), BF16),
            pltpu.VMEM((MODES, channels), F32),
            pltpu.VMEM((MODES, channels), F32),
            pltpu.VMEM((1, channels), F32),
            pltpu.VMEM(fwd.shape, BF16),
            pltpu.VMEM(pair.shape, BF16),
            pltpu.VMEM(back_end.shape, BF16),
            pltpu.VMEM(back_start.shape, BF16),
            dma((8,)), dma((5,)), dma((3,)), dma((2,)), dma((chunks,)), dma((chunks,)), dma((dps,)), dma((dps,)),
            dma((parts,)), dma((parts,)), dma((parts,)), dma((parts,)), dma((chunks,)),
        ],
        compiler_params=pltpu.CompilerParams(
            vmem_limit_bytes=VMEM_LIMIT, collective_id=0, has_side_effects=True
        ),
        name="states",
    )(
        genome_blocks, values[0], gate_one[0], gate_two[0], short_taps, medium_taps, rate, residue.T, long_skip[None],
        fwd, pair, back_end, back_start,
    )

    per_chunk = WIDE // width
    mixed = pl.pallas_call(
        kernel_mixed,
        grid=(chunks,),
        in_specs=[
            smem, chunked(rows), chunked(rows), pl.BlockSpec((count, MODES, WIDE), lambda i: (0, 0, i)),
            pl.BlockSpec((per_chunk, MODES, width), lambda i: (i, 0, 0)),
            chunked(MODES), chunked(MODES),
        ],
        out_specs=chunked(rows),
        out_shape=jax.ShapeDtypeStruct((rows, channels), BF16),
        compiler_params=pltpu.CompilerParams(vmem_limit_bytes=VMEM_LIMIT),
        name="mixed",
    )(genome_blocks, intra, gate_three[0], local, incoming, rate, amplitude)
    return mixed[None]


def solution(mesh):
    return jax.shard_map(
        body,
        mesh=mesh,
        in_specs=(
            P("dp", "seq", None),
            P("dp", "seq", None),
            P("dp", "seq", None),
            P("dp", "seq", None),
            P("dp", None),
            P(),
            P(None, "dp"),
            P(),
            P(),
            P(),
        ),
        out_specs=P("dp", "seq", None),
        check_vma=False,
    )
```
